32 devices in a mesh: group: 4 (over x, core), ctx: 8 (over z, y).
Axes of the slice: x: 2, y: 2, z: 4, core: 2. Of those that a mesh axis runs over, the one named last changes fastest.
Arguments:
- series: bfloat16 [8192, 768], P(('group', 'ctx')), may hold values from -6 to 6
- recon_mask: int32 [8192], P(('group', 'ctx')), may hold values 0 or 1
- mask_token: bfloat16 [768], replicated, may hold values from -4 to 4
- packing_list: int32 [128], P(('group', 'ctx')), may hold values from 0 to 3, as said below
- doc_ids: int32 [4, 2048], P('group', 'ctx'), may hold values from 0 to 3, never falling along the last dimension, each value on 1 to 1280 neighbouring positions
- norm_gain: bfloat16 [768], replicated, may hold values from 0.099609375 to 1.8984375
- w_query: bfloat16 [768, 768], replicated
- w_key: bfloat16 [768, 768], replicated
- w_value: bfloat16 [768, 768], replicated, may hold values from -0.21875 to 0.21875
- w_out: bfloat16 [768, 768], replicated, may hold values from -0.21875 to 0.21875
Outputs:
- encoded: bfloat16 [8192, 768], P(('group', 'ctx'))
The draws below stay inside these ranges and needn't reach their ends.
Inputs may be any that keep to these rules, and one draw needn't show every extreme that they name: `packing_list`: the 4 consecutive entries of each arrival block (one device of the arrival layout) name every packed group exactly once.
All inputs are finite; a program needn't handle non-finite values. No bound on the sum of `recon_mask` on one device may be relied on, other than what follows from the above.
Results may differ from the reference program's by a relative error of at most 0.005.
Values may be sent and summed in bfloat16 or wider, within the bound.
No kernel may reach another device: no remote copies, remote signals or barrier semaphores. Data moves between devices by JAX's collectives and lax.ppermute only.
A program may use at most 128 MiB of HBM per device.

```python
import math
import jax
import jax.numpy as jnp
import numpy as np
from jax import lax

D = 768
HEADS = 12
HD = 64
DOCS = 4
BLK = 64
GROUP_TOK = 2048
DOC_MOST = 1280
TOKENS = 8192
N_GROUP = 4
N_CTX = 8


def draw_packing_list(key, part):
    device_keys = jax.random.split(key, N_GROUP * N_CTX)
    listed = jax.vmap(lambda single: jax.random.permutation(single, N_GROUP))(device_keys)
    return listed.reshape(-1).astype(jnp.int32)


def query_matrix(key):
    return jax.random.normal(jax.random.fold_in(key, 11), (D, D), jnp.float32) / math.sqrt(D)


def draw_w_query(key, part):
    return query_matrix(key).astype(jnp.bfloat16)


def draw_w_key(key, part):
    fresh = jax.random.normal(jax.random.fold_in(key, 12), (D, D), jnp.float32) / math.sqrt(D)
    return fresh.astype(jnp.bfloat16)


def plant(values, stream_key, low, high):
    place = [jax.random.randint(jax.random.fold_in(stream_key, axis), (), 0, length) for axis, length in enumerate(values.shape)]
    longest = values.shape.index(max(values.shape))
    beside = place[:longest] + [(place[longest] + 1) % values.shape[longest]] + place[longest + 1:]
    return values.at[tuple(place)].set(low).at[tuple(beside)].set(high)


def shard_levels(key, shape, cuts, smallest, top_value):
    def one(dim, blocks):
        heights = jax.random.uniform(jax.random.fold_in(jax.random.fold_in(key, 6), dim), (blocks,), jnp.float32, smallest / len(cuts), top_value / len(cuts))
        return jnp.repeat(jnp.exp(heights), shape[dim] // blocks).reshape((-1,) + (1,) * (len(shape) - dim - 1))

    level = one(*cuts[0])
    for cut in cuts[1:]:
        level = level * one(*cut)
    return level


def length_profile(number_of, total, reach, skew):
    loads = [(1 << 20) // math.isqrt(standing ** skew) + 1 for standing in range(2, number_of + 1)]
    rest, counts = total - reach - (number_of - 1), [1] * (number_of - 1)
    while rest > 0:
        movable = [i for i in range(number_of - 1) if counts[i] < reach]
        mass, left = sum([loads[i] for i in movable]), rest
        for i in movable:
            extra = min(reach - counts[i], max(1, left * loads[i] // mass), rest)
            counts[i] = counts[i] + extra
            rest = rest - extra
    return np.array([reach] + counts)


def uneven_parts(own_key, amount, total, most, slope):
    if amount == 2:
        one = jax.random.randint(own_key, (), max(1, total - most), min(most, total - 1) + 1)
        return jnp.stack([one, total - one])
    lengths = jnp.asarray(length_profile(amount, total, most, slope), jnp.int32)
    pairs = (amount - 1) // 2
    donor, taker = lengths[1:1 + 2 * pairs:2], lengths[2:2 + 2 * pairs:2]
    room = jnp.minimum(donor - 1, most - taker)
    shifted = jax.random.randint(jax.random.fold_in(own_key, 1), (pairs,), 0, 1 << 20) % (room + 1)
    lengths = lengths.at[1:1 + 2 * pairs:2].set(donor - shifted).at[2:2 + 2 * pairs:2].set(taker + shifted)
    return lengths[jax.random.permutation(jax.random.fold_in(own_key, 2), amount)]


def centred(stream_key, dims, spread, reach, cuts=(), kind=jnp.bfloat16):
    loudness = shard_levels(stream_key, dims, cuts, -0.22, 0.18) if cuts else 1.0
    drawn = jax.random.normal(stream_key, dims, jnp.float32) * spread * loudness
    return jnp.minimum(jnp.maximum(drawn, -reach), reach).astype(kind)


def setup_inputs(seed: int = 0) -> dict:
    key_list = jax.random.split(jax.random.key(seed), 11)
    return {
        "series": centred(key_list[0], (TOKENS, D), 1.0, 6.0, ((0, 32),)),
        "recon_mask": plant((jax.random.randint(key_list[1], (TOKENS,), 0, 20) < 3).astype(jnp.int32), jax.random.fold_in(key_list[1], 1), 0, 1),
        "mask_token": centred(key_list[2], (D,), 1.0, 4.0),
        "packing_list": draw_packing_list(jax.random.fold_in(key_list[10], 71), 0),
        "doc_ids": jax.vmap(lambda own: jnp.searchsorted(jnp.cumsum(uneven_parts(own, DOCS, GROUP_TOK, DOC_MOST, 0)), jnp.arange(GROUP_TOK), side="right"))(jax.random.split(key_list[4], N_GROUP)).reshape((N_GROUP, GROUP_TOK)).astype(jnp.int32),
        "norm_gain": jnp.clip(1.0 + 0.18 * jax.random.normal(key_list[5], (D,), jnp.float32), 0.099609375, 1.8984375).astype(jnp.bfloat16),
        "w_query": draw_w_query(jax.random.fold_in(key_list[10], 71), 0),
        "w_key": draw_w_key(jax.random.fold_in(key_list[10], 71), 0),
        "w_value": centred(key_list[8], (D, D), D ** -0.5, 0.21875),
        "w_out": centred(key_list[9], (D, D), D ** -0.5, 0.21875),
    }


NEGATIVE = -1e+30

def rms_normed(values, gain):
    widened = values.astype(jnp.float32)
    factor = lax.rsqrt(lax.optimization_barrier(jnp.mean(widened * widened, axis=-1, keepdims=True)) + 1e-06)
    return (widened * factor * gain.astype(jnp.float32)[None, :]).astype(jnp.bfloat16)

def attend_group(arguments, norm_gain, w_query, w_key, w_value, w_out):
    packed, documents = arguments
    group_rows = packed.shape[0]
    normed = rms_normed(packed, norm_gain)
    query = jnp.dot(normed, w_query, preferred_element_type=jnp.float32).astype(jnp.bfloat16)
    keyed = jnp.dot(normed, w_key, preferred_element_type=jnp.float32).astype(jnp.bfloat16)
    valued = jnp.dot(normed, w_value, preferred_element_type=jnp.float32).astype(jnp.bfloat16)
    head_key = keyed.reshape(group_rows, HEADS, HD).astype(jnp.float32)
    head_value = valued.reshape(group_rows, HEADS, HD).astype(jnp.float32)
    block_rows = math.gcd(group_rows, 512)
    block_count = group_rows // block_rows
    query_blocks = query.reshape(block_count, block_rows, HEADS, HD)
    doc_blocks = documents.reshape(block_count, block_rows)

    def one_block(block_args):
        query_block, doc_block = block_args
        scores = jnp.einsum('qhd,khd->hqk', query_block.astype(jnp.float32), head_key) * (1.0 / math.sqrt(HD))
        allowed = (doc_block[:, None] == documents[None, :])[None]
        scores = jnp.where(allowed, scores, NEGATIVE)
        rowmax = lax.optimization_barrier(jnp.max(scores, axis=-1, keepdims=True))
        expo = jnp.where(allowed, jnp.exp(scores - rowmax), 0.0)
        totals = lax.optimization_barrier(jnp.sum(expo, axis=-1))
        weights = lax.optimization_barrier(expo.astype(jnp.bfloat16)).astype(jnp.float32)
        summed = jnp.einsum('hqk,khd->hqd', weights, head_value) / totals[..., None]
        return summed.transpose(1, 0, 2).reshape(block_rows, D).astype(jnp.bfloat16)
    attended = lax.map(one_block, (query_blocks, doc_blocks)).reshape(group_rows, D)
    mixed = jnp.dot(attended, w_out, preferred_element_type=jnp.float32)
    return (packed.astype(jnp.float32) + mixed).astype(jnp.bfloat16)

def reference(series, recon_mask, mask_token, packing_list, doc_ids, norm_gain, w_query, w_key, w_value, w_out):
    masked = jnp.where(recon_mask[:, None] == 1, mask_token[None, :], series)
    pieces = masked.reshape(N_GROUP, N_CTX, N_GROUP, BLK, D)
    targets = packing_list.reshape(N_GROUP, N_CTX, N_GROUP).astype(jnp.int32)
    inverse = jnp.argsort(targets, axis=-1).astype(jnp.int32)
    chosen = jnp.take_along_axis(pieces, inverse[:, :, :, None, None], axis=2)
    packed = chosen.transpose(2, 1, 0, 3, 4).reshape(N_GROUP, GROUP_TOK, D)

    def per_group(group_args):
        return attend_group(group_args, norm_gain, w_query, w_key, w_value, w_out)
    out_packed = lax.map(per_group, (packed, doc_ids))
    by_slot = out_packed.reshape(N_GROUP, N_CTX, N_GROUP, BLK, D).transpose(2, 1, 0, 3, 4)
    arrival = jnp.take_along_axis(by_slot, targets[:, :, :, None, None], axis=2)
    return arrival.reshape(TOKENS, D)
```

```python
import functools
import math

import jax
import jax.numpy as jnp
from jax import lax
from jax.experimental import pallas as pl
from jax.experimental.pallas import tpu as pltpu
from jax.sharding import PartitionSpec as P

HEADS = 12
HD = 64
STEP_HEADS = 4
STEP_COLS = STEP_HEADS * HD
STATE_ROWS = HD + 16
NEGATIVE = -1e30
VMEM_LIMIT = 32 * 1024 * 1024


def whole(shape):
    return pl.BlockSpec(shape, lambda *step: (0,) * len(shape))


def smem():
    return pl.BlockSpec(memory_space=pltpu.SMEM)


def params():
    return pltpu.CompilerParams(vmem_limit_bytes=VMEM_LIMIT)


def piece_of(listing_ref, group, groups):
    place = jnp.int32(0)
    for k in range(groups):
        place = place + jnp.where(listing_ref[k] == group, jnp.int32(k), jnp.int32(0))
    return place


def route_kernel(groups, listing_ref, series_ref, mask_ref, token_ref, *rest):
    out_refs, column_ref = rest[:-1], rest[-1]
    rows, width = series_ref.shape
    piece = rows // groups
    for part in range(rows // 128):
        line = mask_ref[part : part + 1, :].astype(jnp.float32)
        column_ref[part * 128 : (part + 1) * 128, :] = jnp.broadcast_to(line, (128, 128)).T
    own = lax.axis_index("group")
    token = token_ref[...].astype(jnp.float32)
    for r in range(groups):
        place = piece_of(listing_ref, lax.bitwise_xor(own, jnp.int32(r)), groups)
        first = pl.multiple_of(place * piece, piece)
        hidden = column_ref[pl.ds(first, piece), :] > 0.5
        arrived = series_ref[pl.ds(first, piece), :].astype(jnp.float32)
        for lane in range(0, width, 128):
            out_refs[r][:, lane : lane + 128] = jnp.where(
                hidden, token[:, lane : lane + 128], arrived[:, lane : lane + 128]
            ).astype(jnp.bfloat16)


def route(packing_list, series, recon_mask, mask_token, groups):
    rows, width = series.shape
    piece = rows // groups
    return pl.pallas_call(
        functools.partial(route_kernel, groups),
        out_shape=[jax.ShapeDtypeStruct((piece, width), jnp.bfloat16)] * groups,
        in_specs=[smem(), whole((rows, width)), whole((rows // 128, 128)), whole((1, width))],
        out_specs=[whole((piece, width))] * groups,
        grid=(1,),
        scratch_shapes=[pltpu.VMEM((rows, 128), jnp.float32)],
        compiler_params=params(),
        name="route",
    )(packing_list, series, recon_mask.reshape(rows // 128, 128), mask_token.reshape(1, width))


def norm_kernel(count, with_borders, *refs):
    piece_refs, gain_ref = refs[:count], refs[count]
    out_ref = refs[-1]
    piece = piece_refs[0].shape[0]
    gain = gain_ref[...].astype(jnp.float32)
    for i, ref in enumerate(piece_refs):
        widened = ref[...].astype(jnp.float32)
        factor = lax.rsqrt(jnp.mean(widened * widened, axis=-1, keepdims=True) + 1e-06)
        out_ref[i * piece : (i + 1) * piece, :] = (widened * factor * gain).astype(jnp.bfloat16)
    if with_borders:
        docs = refs[count + 1][...]
        width = out_ref.shape[1]
        row = lax.broadcasted_iota(jnp.int32, (8, width), 0)
        lines = jnp.zeros((8, width), jnp.float32)
        for d in (1, 2, 3):
            below = jnp.sum(jnp.where(docs < d, 1.0, 0.0), axis=-1, keepdims=True)
            lines = jnp.where(row == d, below, lines)
        out_ref[count * piece :, :] = lines.astype(jnp.bfloat16)


def norm(pieces, gain, docs=None):
    piece, width = pieces[0].shape
    count = len(pieces)
    rows = count * piece + (8 if docs is not None else 0)
    operands = list(pieces) + [gain.reshape(1, width)]
    if docs is not None:
        operands.append(docs)
    return pl.pallas_call(
        functools.partial(norm_kernel, count, docs is not None),
        out_shape=jax.ShapeDtypeStruct((rows, width), jnp.bfloat16),
        in_specs=[whole(member.shape) for member in operands],
        out_specs=whole((rows, width)),
        grid=(1,),
        compiler_params=params(),
        name="norm",
    )(*operands)


def doc_numbers(borders, place):
    docs = jnp.zeros(place.shape, jnp.float32)
    for d in (1, 2, 3):
        docs = docs + jnp.where(place >= borders[d : d + 1, :], 1.0, 0.0)
    return docs


def places_of(count, piece, groups, shape, axis):
    own = lax.axis_index("group")
    held = lax.broadcasted_iota(jnp.int32, shape, axis)
    source = lax.bitwise_xor(held // piece, own)
    return (source * piece + held % piece).astype(jnp.float32)


def attend(x, caps, key_weight, value_weight, queries_ref, state, first):
    keys = jnp.dot(x, key_weight, preferred_element_type=jnp.float32).astype(jnp.bfloat16)
    values = jnp.dot(x, value_weight, preferred_element_type=jnp.float32).T.astype(jnp.bfloat16)
    ones = jnp.ones((16, x.shape[0]), jnp.bfloat16)
    after = []
    for h in range(STEP_HEADS):
        pair = h // 2 * 128
        scores = jnp.dot(
            keys[:, pair : pair + 128], queries_ref[h], preferred_element_type=jnp.float32
        )
        scores = jnp.minimum(scores, caps)
        top = jnp.max(scores, axis=0, keepdims=True)
        if not first:
            top = jnp.maximum(top, state[h][1])
        weights = jnp.exp(scores - top).astype(jnp.bfloat16)
        widened = jnp.concatenate([values[h * HD : (h + 1) * HD], ones], axis=0)
        sums = jnp.dot(widened, weights, preferred_element_type=jnp.float32)
        if not first:
            sums = sums + state[h][0] * jnp.exp(state[h][1] - top)
        after.append((sums, top))
    return after


def load_state(state_ref):
    return [
        (state_ref[h], state_ref[h, HD + 8 : HD + 9, :]) for h in range(STEP_HEADS)
    ]


def store_state(state_ref, state):
    for h in range(STEP_HEADS):
        sums, top = state[h]
        state_ref[h, : HD + 8, :] = sums[: HD + 8]
        state_ref[h, HD + 8 :, :] = jnp.broadcast_to(top, (8, top.shape[1]))


def caps_of(borders, query_docs, piece, groups, rows):
    place = places_of(rows, piece, groups, (rows, rows), 0)
    return jnp.where(doc_numbers(borders, place) == query_docs, jnp.float32(3e38), NEGATIVE)


def own_kernel(
    piece, groups, a_ref, b_ref, wq_ref, wk_ref, wv_ref, queries_ref, docs_ref, state_ref, caps_ref
):
    half = b_ref.shape[0]
    rows = 2 * half
    x = jnp.concatenate([a_ref[:half, :], b_ref[...]], axis=0)

    @pl.when(pl.program_id(0) == 0)
    def first_step():
        borders = a_ref[half:, :rows].astype(jnp.float32)
        place = places_of(rows, piece, groups, (8, rows), 1)
        docs = jnp.zeros((8, rows), jnp.float32)
        for d in (1, 2, 3):
            docs = docs + jnp.where(place >= borders[d : d + 1, :], 1.0, 0.0)
        docs_ref[...] = docs
        caps_ref[...] = caps_of(borders, docs[0:1, :], piece, groups, rows)

    queries = jnp.dot(x, wq_ref[...], preferred_element_type=jnp.float32)
    queries = (queries.astype(jnp.bfloat16).astype(jnp.float32) * (1.0 / math.sqrt(HD))).T
    queries = queries.astype(jnp.bfloat16)
    blank = jnp.zeros((HD, rows), jnp.bfloat16)
    for h in range(STEP_HEADS):
        own = queries[h * HD : (h + 1) * HD]
        queries_ref[h] = jnp.concatenate([own, blank] if h % 2 == 0 else [blank, own], axis=0)
    store_state(
        state_ref, attend(x, caps_ref[...], wk_ref[...], wv_ref[...], queries_ref, None, True)
    )


def fold(piece, groups, sources, docs_ref, caps_ref, wk_ref, wv_ref, queries_ref, state):
    half = sources[0][1].shape[0]
    rows = 2 * half
    for i, (a_ref, b_ref) in enumerate(sources):

        @pl.when(pl.program_id(0) == 0)
        def first_step():
            borders = a_ref[half:, :rows].astype(jnp.float32)
            caps_ref[i] = caps_of(borders, docs_ref[0:1, :], piece, groups, rows)

        x = jnp.concatenate([a_ref[:half, :], b_ref[...]], axis=0)
        state = attend(x, caps_ref[i], wk_ref[...], wv_ref[...], queries_ref, state, False)
    return state


def chunk_kernel(
    piece, groups, count, queries_ref, docs_ref, wk_ref, wv_ref, state_in_ref, *rest
):
    source_refs, state_ref, caps_ref = rest[: 2 * count], rest[2 * count], rest[2 * count + 1]
    sources = [(source_refs[2 * i], source_refs[2 * i + 1]) for i in range(count)]
    state = fold(
        piece, groups, sources, docs_ref, caps_ref, wk_ref, wv_ref, queries_ref, load_state(state_in_ref)
    )
    store_state(state_ref, state)


def last_kernel(
    piece, groups, queries_ref, docs_ref, wk_ref, wv_ref, state_in_ref, a_ref, b_ref, wo_ref, *rest
):
    piece_refs, out_refs = rest[:groups], rest[groups : 2 * groups]
    caps_ref, total_ref = rest[2 * groups], rest[2 * groups + 1]
    state = fold(
        piece, groups, [(a_ref, b_ref)], docs_ref, caps_ref, wk_ref, wv_ref, queries_ref, load_state(state_in_ref)
    )
    attended = jnp.concatenate(
        [(sums[:HD] / sums[HD : HD + 1]) for sums, top in state], axis=0
    ).T.astype(jnp.bfloat16)
    mixed = jnp.dot(attended, wo_ref[...], preferred_element_type=jnp.float32)
    step, last = pl.program_id(0), pl.num_programs(0) - 1

    @pl.when(step == 0)
    def start():
        total_ref[...] = mixed

    @pl.when(jnp.logical_and(step > 0, step < last))
    def middle():
        total_ref[...] += mixed

    @pl.when(step == last)
    def finish():
        summed = total_ref[...] + mixed
        for r in range(groups):
            out_refs[r][...] = (
                piece_refs[r][...].astype(jnp.float32) + summed[r * piece : (r + 1) * piece]
            ).astype(jnp.bfloat16)


def column_block(width):
    return pl.BlockSpec((width, STEP_COLS), lambda step: (0, step))


def queries_block(rows):
    return pl.BlockSpec((STEP_HEADS, 2 * HD, rows), lambda step: (step, 0, 0))


def state_block(rows):
    return pl.BlockSpec((STEP_HEADS, STATE_ROWS, rows), lambda step: (step, 0, 0))


def own_call(a, b, w_query, w_key, w_value, piece, groups):
    rows, width = 2 * b.shape[0], b.shape[1]
    return pl.pallas_call(
        functools.partial(own_kernel, piece, groups),
        out_shape=[
            jax.ShapeDtypeStruct((HEADS, 2 * HD, rows), jnp.bfloat16),
            jax.ShapeDtypeStruct((8, rows), jnp.float32),
            jax.ShapeDtypeStruct((HEADS, STATE_ROWS, rows), jnp.float32),
        ],
        in_specs=[whole(a.shape), whole(b.shape)] + [column_block(width)] * 3,
        out_specs=[queries_block(rows), whole((8, rows)), state_block(rows)],
        grid=(HEADS // STEP_HEADS,),
        scratch_shapes=[pltpu.VMEM((rows, rows), jnp.float32)],
        compiler_params=params(),
        name="own_rows",
    )(a, b, w_query, w_key, w_value)


def chunk_call(queries, docs, w_key, w_value, state, sources, piece, groups):
    rows, width = queries.shape[2], w_key.shape[0]
    flat = [member for source in sources for member in source]
    return pl.pallas_call(
        functools.partial(chunk_kernel, piece, groups, len(sources)),
        out_shape=jax.ShapeDtypeStruct(state.shape, jnp.float32),
        in_specs=[queries_block(rows), whole(docs.shape), column_block(width), column_block(width), state_block(rows)]
        + [whole(member.shape) for member in flat],
        out_specs=state_block(rows),
        grid=(HEADS // STEP_HEADS,),
        scratch_shapes=[pltpu.VMEM((len(sources), rows, rows), jnp.float32)],
        input_output_aliases={4: 0},
        compiler_params=params(),
        name="received_rows",
    )(queries, docs, w_key, w_value, state, *flat)


def last_call(queries, docs, w_key, w_value, state, a, b, w_out, pieces, piece, groups):
    rows, width = queries.shape[2], w_key.shape[0]
    return pl.pallas_call(
        functools.partial(last_kernel, piece, groups),
        out_shape=[jax.ShapeDtypeStruct((piece, width), jnp.bfloat16)] * groups,
        in_specs=[queries_block(rows), whole(docs.shape), column_block(width), column_block(width), state_block(rows)]
        + [whole(a.shape), whole(b.shape), pl.BlockSpec((STEP_COLS, width), lambda step: (step, 0))]
        + [whole((piece, width))] * groups,
        out_specs=[whole((piece, width))] * groups,
        grid=(HEADS // STEP_HEADS,),
        scratch_shapes=[
            pltpu.VMEM((1, rows, rows), jnp.float32),
            pltpu.VMEM((rows, width), jnp.float32),
        ],
        compiler_params=params(),
        name="last_rows",
    )(queries, docs, w_key, w_value, state, a, b, w_out, *pieces)


def arrange_kernel(groups, listing_ref, *refs):
    piece_refs, out_ref = refs[:groups], refs[groups]
    piece = piece_refs[0].shape[0]
    own = lax.axis_index("group")
    for r in range(groups):
        place = piece_of(listing_ref, lax.bitwise_xor(own, jnp.int32(r)), groups)
        out_ref[pl.ds(pl.multiple_of(place * piece, piece), piece), :] = piece_refs[r][...]


def arrange(packing_list, pieces):
    groups, (piece, width) = len(pieces), pieces[0].shape
    return pl.pallas_call(
        functools.partial(arrange_kernel, groups),
        out_shape=jax.ShapeDtypeStruct((groups * piece, width), jnp.bfloat16),
        in_specs=[smem()] + [whole((piece, width))] * groups,
        out_specs=whole((groups * piece, width)),
        grid=(1,),
        compiler_params=params(),
        name="arrange",
    )(packing_list, *pieces)


def exchange(pieces):
    groups = len(pieces)
    return [pieces[0]] + [
        lax.ppermute(pieces[r], "group", [(i, i ^ r) for i in range(groups)])
        for r in range(1, groups)
    ]


def on_device(
    series, recon_mask, mask_token, packing_list, doc_ids, norm_gain, w_query, w_key, w_value, w_out
):
    groups, shards = lax.axis_size("group"), lax.axis_size("ctx")
    rows, width = series.shape
    piece = rows // groups
    ring = list(range(0, shards, 2)) + list(range(shards - 1, 0, -2))
    onward = [(ring[i], ring[(i + 1) % shards]) for i in range(shards)]
    backward = [(there, here) for here, there in onward]

    pieces = exchange(route(packing_list, series, recon_mask, mask_token, groups))
    a = norm(pieces[: groups // 2], norm_gain, doc_ids)
    b = norm(pieces[groups // 2 :], norm_gain)
    queries, docs, state = own_call(a, b, w_query, w_key, w_value, piece, groups)
    before, after = (a, b), (a, b)
    for step in range(1, shards // 2):
        before = tuple(lax.ppermute(member, "ctx", onward) for member in before)
        after = tuple(lax.ppermute(member, "ctx", backward) for member in after)
        state = chunk_call(
            queries, docs, w_key, w_value, state, (before, after), piece, groups
        )
    far_a = lax.ppermute(before[0], "ctx", onward)
    far_b = lax.ppermute(after[1], "ctx", backward)
    done = last_call(
        queries, docs, w_key, w_value, state, far_a, far_b, w_out, pieces, piece, groups
    )
    return arrange(packing_list, exchange(done))


def solution(mesh):
    in_specs = (
        P(("group", "ctx"), None),
        P(("group", "ctx")),
        P(),
        P(("group", "ctx")),
        P("group", "ctx"),
        P(),
        P(),
        P(),
        P(),
        P(),
    )
    out_specs = P(("group", "ctx"), None)
    return jax.shard_map(
        on_device, mesh=mesh, in_specs=in_specs, out_specs=out_specs, check_vma=False
    )
```

```python
import functools
import math

import jax
import jax.numpy as jnp
from jax import lax
from jax.experimental import pallas as pl
from jax.experimental.pallas import tpu as pltpu
from jax.sharding import PartitionSpec as P

HEADS = 12
HD = 64
STEP_HEADS = 4
STEP_COLS = STEP_HEADS * HD
STATE_ROWS = HD + 16
BIG = 3.3895313892515355e38
LARGEST = 1e30
LOG2E = 1.4426950408889634
HALVES = True
VMEM_LIMIT = 32 * 1024 * 1024


def whole(shape):
    return pl.BlockSpec(shape, lambda *step: (0,) * len(shape))


def smem():
    return pl.BlockSpec(memory_space=pltpu.SMEM)


def params():
    return pltpu.CompilerParams(vmem_limit_bytes=VMEM_LIMIT)


def piece_of(listing_ref, group, groups):
    place = jnp.int32(0)
    for k in range(groups):
        place = place + jnp.where(listing_ref[k] == group, jnp.int32(k), jnp.int32(0))
    return place


def route_kernel(groups, listing_ref, series_ref, mask_ref, token_ref, *rest):
    out_refs, column_ref = rest[:-1], rest[-1]
    rows, width = series_ref.shape
    piece = rows // groups
    for part in range(rows // 128):
        line = mask_ref[part : part + 1, :].astype(jnp.float32)
        column_ref[part * 128 : (part + 1) * 128, :] = jnp.broadcast_to(line, (128, 128)).T
    own = lax.axis_index("group")
    token = token_ref[...].astype(jnp.float32)
    for r in range(groups):
        place = piece_of(listing_ref, lax.bitwise_xor(own, jnp.int32(r)), groups)
        first = pl.multiple_of(place * piece, piece)
        hidden = column_ref[pl.ds(first, piece), :] > 0.5
        arrived = series_ref[pl.ds(first, piece), :].astype(jnp.float32)
        for lane in range(0, width, 128):
            out_refs[r][:, lane : lane + 128] = jnp.where(
                hidden, token[:, lane : lane + 128], arrived[:, lane : lane + 128]
            ).astype(jnp.bfloat16)


def route(packing_list, series, recon_mask, mask_token, groups):
    rows, width = series.shape
    piece = rows // groups
    return pl.pallas_call(
        functools.partial(route_kernel, groups),
        out_shape=[jax.ShapeDtypeStruct((piece, width), jnp.bfloat16)] * groups,
        in_specs=[smem(), whole((rows, width)), whole((rows // 128, 128)), whole((1, width))],
        out_specs=[whole((piece, width))] * groups,
        grid=(1,),
        scratch_shapes=[pltpu.VMEM((rows, 128), jnp.float32)],
        compiler_params=params(),
        name="route",
    )(packing_list, series, recon_mask.reshape(rows // 128, 128), mask_token.reshape(1, width))


def norm_kernel(count, with_borders, *refs):
    piece_refs, gain_ref = refs[:count], refs[count]
    out_ref = refs[-1]
    piece = piece_refs[0].shape[0]
    gain = gain_ref[...].astype(jnp.float32)
    for i, ref in enumerate(piece_refs):
        widened = ref[...].astype(jnp.float32)
        factor = lax.rsqrt(jnp.mean(widened * widened, axis=-1, keepdims=True) + 1e-06)
        out_ref[i * piece : (i + 1) * piece, :] = (widened * factor * gain).astype(jnp.bfloat16)
    if with_borders:
        docs = refs[count + 1][...]
        width = out_ref.shape[1]
        row = lax.broadcasted_iota(jnp.int32, (8, width), 0)
        lines = jnp.zeros((8, width), jnp.float32)
        for d in (1, 2, 3):
            below = jnp.sum(jnp.where(docs < d, 1.0, 0.0), axis=-1, keepdims=True)
            lines = jnp.where(row == d, below, lines)
        out_ref[count * piece :, :] = lines.astype(jnp.bfloat16)


def norm(pieces, gain, docs=None):
    piece, width = pieces[0].shape
    count = len(pieces)
    rows = count * piece + (8 if docs is not None else 0)
    operands = list(pieces) + [gain.reshape(1, width)]
    if docs is not None:
        operands.append(docs)
    return pl.pallas_call(
        functools.partial(norm_kernel, count, docs is not None),
        out_shape=jax.ShapeDtypeStruct((rows, width), jnp.bfloat16),
        in_specs=[whole(member.shape) for member in operands],
        out_specs=whole((rows, width)),
        grid=(1,),
        compiler_params=params(),
        name="norm",
    )(*operands)


def borders_of(ref, first):
    return ref[first : first + 8, :].astype(jnp.float32)


def places_of(count, piece, shape, axis):
    own = lax.axis_index("group")
    held = lax.broadcasted_iota(jnp.int32, shape, axis)
    source = lax.bitwise_xor(held // piece, own)
    return (source * piece + held % piece).astype(jnp.float32)


def doc_numbers(borders, place):
    docs = jnp.zeros(place.shape, jnp.float32)
    for d in (1, 2, 3):
        docs = docs + jnp.where(place >= borders[d : d + 1, : place.shape[1]], 1.0, 0.0)
    return docs


def key_extras(borders, rows, piece):
    docs = doc_numbers(borders, places_of(rows, piece, (rows, 128), 0))
    column = lax.rem(lax.broadcasted_iota(jnp.int32, (rows, 128), 1), HD)
    named = jnp.where(docs == column.astype(jnp.float32), 1.0, 0.0)
    flags = jnp.where(column < 7, 1.0, 0.0)
    return jnp.where(column < 4, named, flags).astype(jnp.bfloat16)


def load_rows(parts):
    return jnp.concatenate([ref[first : first + count, :] for ref, first, count in parts], axis=0)


def scores_of(keys, extras, queries):
    low = lax.broadcasted_iota(jnp.int32, extras.shape, 1) < HD
    scores = []
    for h in range(STEP_HEADS):
        pair = keys[:, h // 2 * 128 : h // 2 * 128 + 128]
        mixed = jnp.where(low, pair, extras) if h % 2 == 0 else jnp.where(low, extras, pair)
        scores.append(jnp.dot(mixed, queries[h], preferred_element_type=jnp.float32))
    return scores


def with_ones(values, h):
    ones = jnp.ones((16, values.shape[1]), jnp.bfloat16)
    return jnp.concatenate([values[h * HD : (h + 1) * HD], ones], axis=0)


def project(x, weight_ref, j):
    columns = weight_ref[:, j * STEP_COLS : (j + 1) * STEP_COLS]
    return jnp.dot(x, columns, preferred_element_type=jnp.float32)


def own_kernel(piece, parts, borders_at, *refs):
    row_refs, (wq_ref, wk_ref, wv_ref, queries_ref, state_ref) = refs[:-5], refs[-5:]
    x = load_rows([(row_refs[i], first, count) for i, first, count in parts])
    rows = x.shape[0]
    borders = borders_of(row_refs[borders_at[0]], borders_at[1])
    docs = doc_numbers(borders, places_of(rows, piece, (8, rows), 1))
    row = lax.broadcasted_iota(jnp.int32, (HD, rows), 0)
    differs = jnp.where(docs[0:1, :] == row.astype(jnp.float32), 0.0, -BIG)
    mask_rows = jnp.where(row < 4, differs, 0.0)
    extras = key_extras(borders, rows, piece)
    for j in range(HEADS // STEP_HEADS):
        queries = project(x, wq_ref, j).astype(jnp.bfloat16).astype(jnp.float32)
        queries = (queries * (1.0 / math.sqrt(HD))).T.astype(jnp.bfloat16)
        keys = project(x, wk_ref, j).astype(jnp.bfloat16)
        values = project(x, wv_ref, j).T.astype(jnp.bfloat16)

        def stacked(h, rest):
            own = queries[h * HD : (h + 1) * HD]
            return jnp.concatenate([own, rest] if h % 2 == 0 else [rest, own], axis=0)

        plain = mask_rows.astype(jnp.bfloat16)
        scores = scores_of(keys, extras, [stacked(h, plain) for h in range(STEP_HEADS)])
        tops = [jnp.max(member, axis=0, keepdims=True) for member in scores]
        weights = [
            jnp.exp2((member - top) * LOG2E).astype(jnp.bfloat16)
            for member, top in zip(scores, tops)
        ]
        sums = [
            jnp.dot(with_ones(values, h), weights[h], preferred_element_type=jnp.float32)
            for h in range(STEP_HEADS)
        ]
        for h in range(STEP_HEADS):
            upper = tops[h].astype(jnp.bfloat16).astype(jnp.float32)
            middle = (tops[h] - upper).astype(jnp.bfloat16).astype(jnp.float32)
            lower = tops[h] - upper - middle
            rest = jnp.where(row == 4, -upper, mask_rows)
            rest = jnp.where(row == 5, -middle, rest)
            rest = jnp.where(row == 6, -lower, rest)
            queries_ref[j * STEP_HEADS + h] = stacked(h, rest.astype(jnp.bfloat16))
            state_ref[j * STEP_HEADS + h, : HD + 8, :] = sums[h][: HD + 8]
            state_ref[j * STEP_HEADS + h, HD + 8 :, :] = jnp.zeros((8, rows), jnp.float32)


def fold(piece, sources, queries_ref, wk_ref, wv_ref, state_ref, finish):
    x = jnp.concatenate([load_rows(parts) for parts, _, _ in sources], axis=0)
    extras = jnp.concatenate(
        [
            key_extras(borders_of(ref, first), sum(count for _, _, count in parts), piece)
            for parts, ref, first in sources
        ],
        axis=0,
    )
    for j in range(HEADS // STEP_HEADS):
        heads = [j * STEP_HEADS + h for h in range(STEP_HEADS)]
        keys = project(x, wk_ref, j).astype(jnp.bfloat16)
        values = project(x, wv_ref, j).T.astype(jnp.bfloat16)
        scores = scores_of(keys, extras, [queries_ref[head] for head in heads])
        weights = [jnp.exp2(member * LOG2E).astype(jnp.bfloat16) for member in scores]
        sums = [
            state_ref[head, : HD + 8, :]
            + jnp.dot(with_ones(values, h), weights[h], preferred_element_type=jnp.float32)[: HD + 8]
            for h, head in enumerate(heads)
        ]
        largest = functools.reduce(jnp.maximum, [member[HD : HD + 8] for member in sums])
        excess = functools.reduce(jnp.maximum, [state_ref[head, HD + 8 :, :] for head in heads])
        usual = jnp.logical_and(jnp.max(largest) < LARGEST, jnp.max(excess) <= 0.0)

        @pl.when(usual)
        def plain():
            finish(j, sums, None)

        @pl.when(jnp.logical_not(usual))
        def again():
            scores = scores_of(keys, extras, [queries_ref[head] for head in heads])
            tops, sums = [], []
            for h, head in enumerate(heads):
                before = state_ref[head, HD + 8 : HD + 9, :]
                top = jnp.maximum(before, jnp.max(scores[h], axis=0, keepdims=True))
                weights = jnp.exp2((scores[h] - top) * LOG2E).astype(jnp.bfloat16)
                added = jnp.dot(with_ones(values, h), weights, preferred_element_type=jnp.float32)
                factor = jnp.exp2((before - top) * LOG2E)
                sums.append(state_ref[head, : HD + 8, :] * factor + added[: HD + 8])
                tops.append(jnp.broadcast_to(top, (8, top.shape[1])))
            finish(j, sums, tops)


def named_sources(row_refs, layout):
    return [
        ([(row_refs[i], first, count) for i, first, count in parts], row_refs[at], first_border)
        for parts, (at, first_border) in layout
    ]


def chunk_kernel(piece, layout, queries_ref, wk_ref, wv_ref, old_ref, *rest):
    row_refs, state_ref = rest[:-1], rest[-1]

    def finish(j, sums, tops):
        for h in range(STEP_HEADS):
            head = j * STEP_HEADS + h
            state_ref[head, : HD + 8, :] = sums[h]
            if tops is None:
                state_ref[head, HD + 8 :, :] = jnp.zeros((8, sums[h].shape[1]), jnp.float32)
            else:
                state_ref[head, HD + 8 :, :] = tops[h]

    fold(piece, named_sources(row_refs, layout), queries_ref, wk_ref, wv_ref, old_ref, finish)


def last_kernel(groups, piece, layout, queries_ref, wk_ref, wv_ref, old_ref, wo_ref, *rest):
    row_refs = rest[: -2 * groups - 1]
    piece_refs, out_refs = rest[-2 * groups - 1 : -groups - 1], rest[-groups - 1 : -1]
    attended_ref = rest[-1]

    def finish(j, sums, tops):
        for h in range(STEP_HEADS):
            first = (j * STEP_HEADS + h) * HD
            attended_ref[first : first + HD, :] = sums[h][:HD] / sums[h][HD : HD + 1]

    fold(piece, named_sources(row_refs, layout), queries_ref, wk_ref, wv_ref, old_ref, finish)
    attended = attended_ref[...].T.astype(jnp.bfloat16)
    mixed = jnp.dot(attended, wo_ref[...], preferred_element_type=jnp.float32)
    for r in range(groups):
        out_refs[r][...] = (
            piece_refs[r][...].astype(jnp.float32) + mixed[r * piece : (r + 1) * piece]
        ).astype(jnp.bfloat16)


def vmem(count):
    return [pl.BlockSpec(memory_space=pltpu.VMEM)] * count


def cost(us):
    return pl.CostEstimate(flops=int(us * 1.1e9), bytes_accessed=0, transcendentals=0)


def own_call(members, layout, w_query, w_key, w_value, piece, rows):
    parts, borders_at = layout
    return pl.pallas_call(
        functools.partial(own_kernel, piece, parts, borders_at),
        out_shape=[
            jax.ShapeDtypeStruct((HEADS, 2 * HD, rows), jnp.bfloat16),
            jax.ShapeDtypeStruct((HEADS, STATE_ROWS, rows), jnp.float32),
        ],
        in_specs=vmem(len(members) + 3),
        out_specs=vmem(2),
        compiler_params=params(),
        cost_estimate=cost(3.0),
        name="own_rows",
    )(*members, w_query, w_key, w_value)


def chunk_call(queries, w_key, w_value, state, members, layout, piece):
    return pl.pallas_call(
        functools.partial(chunk_kernel, piece, layout),
        out_shape=jax.ShapeDtypeStruct(state.shape, jnp.float32),
        in_specs=vmem(4 + len(members)),
        out_specs=vmem(1)[0],
        compiler_params=params(),
        cost_estimate=cost(3.5),
        name="received_rows",
    )(queries, w_key, w_value, state, *members)


def last_call(queries, w_key, w_value, state, w_out, members, layout, pieces, piece):
    groups, width = len(pieces), w_key.shape[0]
    rows = queries.shape[2]
    return pl.pallas_call(
        functools.partial(last_kernel, groups, piece, layout),
        out_shape=[jax.ShapeDtypeStruct((piece, width), jnp.bfloat16)] * groups,
        in_specs=vmem(5 + len(members) + groups),
        out_specs=vmem(groups),
        scratch_shapes=[pltpu.VMEM((HEADS * HD, rows), jnp.float32)],
        compiler_params=params(),
        cost_estimate=cost(3.0),
        name="last_rows",
    )(queries, w_key, w_value, state, w_out, *members, *pieces)


def arrange_kernel(groups, listing_ref, *refs):
    piece_refs, out_ref = refs[:groups], refs[groups]
    piece = piece_refs[0].shape[0]
    own = lax.axis_index("group")
    for r in range(groups):
        place = piece_of(listing_ref, lax.bitwise_xor(own, jnp.int32(r)), groups)
        out_ref[pl.ds(pl.multiple_of(place * piece, piece), piece), :] = piece_refs[r][...]


def arrange(packing_list, pieces):
    groups, (piece, width) = len(pieces), pieces[0].shape
    return pl.pallas_call(
        functools.partial(arrange_kernel, groups),
        out_shape=jax.ShapeDtypeStruct((groups * piece, width), jnp.bfloat16),
        in_specs=[smem()] + [whole((piece, width))] * groups,
        out_specs=whole((groups * piece, width)),
        grid=(1,),
        compiler_params=params(),
        name="arrange",
    )(packing_list, *pieces)


def exchange(pieces):
    groups = len(pieces)
    return [pieces[0]] + [
        lax.ppermute(pieces[r], "group", [(i, i ^ r) for i in range(groups)])
        for r in range(1, groups)
    ]


def on_device(
    series, recon_mask, mask_token, packing_list, doc_ids, norm_gain, w_query, w_key, w_value, w_out
):
    groups, shards = lax.axis_size("group"), lax.axis_size("ctx")
    rows, width = series.shape
    piece = rows // groups
    ring = list(range(0, shards, 2)) + list(range(shards - 1, 0, -2))
    onward = [(ring[i], ring[(i + 1) % shards]) for i in range(shards)]
    backward = [(there, here) for here, there in onward]

    pieces = exchange(route(packing_list, series, recon_mask, mask_token, groups))
    half = rows // 2
    if HALVES:
        own = (
            norm(pieces[: groups // 2], norm_gain, doc_ids),
            norm(pieces[groups // 2 :], norm_gain),
        )
        parts = [(0, 0, half), (1, 0, half)]
        own_layout = (parts, (0, half))
        pair_layout = (own_layout, ([(2, 0, half), (3, 0, half)], (2, half)))
        far_layout = (own_layout,)
    else:
        own = (norm(pieces, norm_gain, doc_ids),)
        own_layout = ([(0, 0, rows)], (0, rows))
        pair_layout = (own_layout, ([(1, 0, rows)], (1, rows)))
        far_layout = (([(0, 0, half), (1, 0, half)], (1, half)),)
    queries, state = own_call(own, own_layout, w_query, w_key, w_value, piece, rows)
    before, after = own, own
    for step in range(1, shards // 2):
        before = tuple(lax.ppermute(member, "ctx", onward) for member in before)
        after = tuple(lax.ppermute(member, "ctx", backward) for member in after)
        state = chunk_call(queries, w_key, w_value, state, before + after, pair_layout, piece)
    if HALVES:
        far = (
            lax.ppermute(before[0], "ctx", onward),
            lax.ppermute(after[1], "ctx", backward),
        )
    else:
        far = (
            lax.ppermute(before[0][:half], "ctx", onward),
            lax.ppermute(after[0][half:], "ctx", backward),
        )
    done = last_call(queries, w_key, w_value, state, w_out, far, far_layout, pieces, piece)
    return arrange(packing_list, exchange(done))


def solution(mesh):
    in_specs = (
        P(("group", "ctx"), None),
        P(("group", "ctx")),
        P(),
        P(("group", "ctx")),
        P("group", "ctx"),
        P(),
        P(),
        P(),
        P(),
        P(),
    )
    out_specs = P(("group", "ctx"), None)
    return jax.shard_map(
        on_device, mesh=mesh, in_specs=in_specs, out_specs=out_specs, check_vma=False
    )
```

```python
import functools
import math

import jax
import jax.numpy as jnp
from jax import lax
from jax.experimental import pallas as pl
from jax.experimental.pallas import tpu as pltpu
from jax.sharding import PartitionSpec as P

HEADS = 12
HD = 64
STEP_HEADS = 4
STEP_COLS = STEP_HEADS * HD
STATE_ROWS = HD + 16
BIG = 3.3895313892515355e38
LARGEST = 1e30
LOG2E = 1.4426950408889634
VMEM_LIMIT = 32 * 1024 * 1024
LARGE = 56 * 1024 * 1024


def vmem(count):
    return [pl.BlockSpec(memory_space=pltpu.VMEM)] * count


def anywhere(count):
    return [pl.BlockSpec(memory_space=pl.ANY)] * count


def smem():
    return pl.BlockSpec(memory_space=pltpu.SMEM)


def params(limit=VMEM_LIMIT):
    return pltpu.CompilerParams(vmem_limit_bytes=limit)


def cost(us):
    return pl.CostEstimate(flops=int(us * 1.1e9), bytes_accessed=0, transcendentals=0)


def piece_of(listing_ref, group, groups):
    place = jnp.int32(0)
    for k in range(groups):
        place = place + jnp.where(listing_ref[k] == group, jnp.int32(k), jnp.int32(0))
    return place


def route_kernel(groups, listing_ref, series_ref, mask_ref, token_ref, *rest):
    out_refs, (held_ref, lines_ref, word_ref, column_ref, sems) = rest[:groups], rest[groups:]
    piece, width = out_refs[0].shape
    own = lax.axis_index("group")
    copies = [
        pltpu.make_async_copy(mask_ref, lines_ref, sems.at[groups]),
        pltpu.make_async_copy(token_ref, word_ref, sems.at[groups + 1]),
    ]
    firsts = []
    for r in range(groups):
        place = piece_of(listing_ref, lax.bitwise_xor(own, jnp.int32(r)), groups)
        first = pl.multiple_of(place * piece, piece)
        firsts.append(first)
        copies.append(
            pltpu.make_async_copy(
                series_ref.at[pl.ds(first, piece), :],
                held_ref.at[r * piece : (r + 1) * piece, :],
                sems.at[r],
            )
        )
    for copy in copies:
        copy.start()
    copies[0].wait()
    for part in range(lines_ref.shape[0]):
        line = lines_ref[part : part + 1, :].astype(jnp.float32)
        column_ref[part * 128 : (part + 1) * 128, :] = jnp.broadcast_to(line, (128, 128)).T
    copies[1].wait()
    token = word_ref[...].astype(jnp.float32).reshape(1, width)
    for r in range(groups):
        copies[2 + r].wait()
        hidden = column_ref[pl.ds(firsts[r], piece), :] > 0.5
        arrived = held_ref[r * piece : (r + 1) * piece, :].astype(jnp.float32)
        for lane in range(0, width, 128):
            out_refs[r][:, lane : lane + 128] = jnp.where(
                hidden, token[:, lane : lane + 128], arrived[:, lane : lane + 128]
            ).astype(jnp.bfloat16)


def route(packing_list, series, recon_mask, mask_token, groups):
    rows, width = series.shape
    piece = rows // groups
    return pl.pallas_call(
        functools.partial(route_kernel, groups),
        out_shape=[jax.ShapeDtypeStruct((piece, width), jnp.bfloat16)] * groups,
        in_specs=[smem()] + anywhere(3),
        out_specs=vmem(groups),
        scratch_shapes=[
            pltpu.VMEM((rows, width), jnp.bfloat16),
            pltpu.VMEM((rows // 128, 128), jnp.int32),
            pltpu.VMEM((width,), jnp.bfloat16),
            pltpu.VMEM((rows, 128), jnp.float32),
            pltpu.SemaphoreType.DMA((groups + 2,)),
        ],
        compiler_params=params(LARGE),
        cost_estimate=cost(1.5),
        name="route",
    )(packing_list, series, recon_mask.reshape(rows // 128, 128), mask_token)


def stage_kernel(count, turned, *refs):
    from_refs, to_refs = refs[:count], refs[count + 1 : 2 * count + 1]
    scratch, sems = refs[2 * count + 1 : -1], refs[-1]
    copies = []
    for i in range(count):
        target = scratch[0] if i == turned else to_refs[i]
        copies.append(pltpu.make_async_copy(from_refs[i], target, sems.at[i]))
    for copy in copies:
        copy.start()
    for copy in copies:
        copy.wait()
    if turned is not None:
        width = to_refs[turned].shape[0]
        for lane in range(0, width, 256):
            to_refs[turned][lane : lane + 256, :] = (
                scratch[0][:, lane : lane + 256].astype(jnp.float32).T.astype(jnp.bfloat16)
            )


def stage(weights, turned, behind, us):
    count = len(weights)
    scratch = [pltpu.VMEM(weights[turned].shape, jnp.bfloat16)] if turned is not None else []
    return pl.pallas_call(
        functools.partial(stage_kernel, count, turned),
        out_shape=[jax.ShapeDtypeStruct(member.shape, member.dtype) for member in weights],
        in_specs=anywhere(count + 1),
        out_specs=vmem(count),
        scratch_shapes=scratch + [pltpu.SemaphoreType.DMA((count,))],
        compiler_params=params(),
        cost_estimate=cost(us),
        name="stage",
    )(*weights, behind)


def norm_kernel(count, with_borders, *refs):
    piece_refs, gain_ref = refs[:count], refs[count]
    out_ref = refs[-1]
    piece, width = piece_refs[0].shape
    gain = gain_ref[...].astype(jnp.float32).reshape(1, width)
    for i, ref in enumerate(piece_refs):
        widened = ref[...].astype(jnp.float32)
        factor = lax.rsqrt(jnp.mean(widened * widened, axis=-1, keepdims=True) + 1e-06)
        out_ref[i * piece : (i + 1) * piece, :] = (widened * factor * gain).astype(jnp.bfloat16)
    if with_borders:
        docs = refs[count + 1][...]
        row = lax.broadcasted_iota(jnp.int32, (8, width), 0)
        lines = jnp.zeros((8, width), jnp.float32)
        for d in (1, 2, 3):
            below = jnp.sum(jnp.where(docs < d, 1.0, 0.0), axis=-1, keepdims=True)
            lines = jnp.where(row == d, below, lines)
        out_ref[count * piece :, :] = lines.astype(jnp.bfloat16)


def norm(pieces, gain, docs=None, behind=()):
    piece, width = pieces[0].shape
    count = len(pieces)
    rows = count * piece + (8 if docs is not None else 0)
    operands = list(pieces) + [gain] + ([docs] if docs is not None else [])
    return pl.pallas_call(
        functools.partial(norm_kernel, count, docs is not None),
        out_shape=jax.ShapeDtypeStruct((rows, width), jnp.bfloat16),
        in_specs=vmem(len(operands)) + anywhere(len(behind)),
        out_specs=vmem(1)[0],
        compiler_params=params(),
        cost_estimate=cost(0.3),
        name="norm",
    )(*operands, *behind)


def borders_of(ref, first):
    return ref[first : first + 8, :].astype(jnp.float32)


def places_of(count, piece, shape, axis):
    own = lax.axis_index("group")
    held = lax.broadcasted_iota(jnp.int32, shape, axis)
    source = lax.bitwise_xor(held // piece, own)
    return (source * piece + held % piece).astype(jnp.float32)


def doc_numbers(borders, place):
    docs = jnp.zeros(place.shape, jnp.float32)
    for d in (1, 2, 3):
        docs = docs + jnp.where(place >= borders[d : d + 1, : place.shape[1]], 1.0, 0.0)
    return docs


def key_extras(borders, rows, piece):
    docs = doc_numbers(borders, places_of(rows, piece, (rows, 128), 0))
    column = lax.rem(lax.broadcasted_iota(jnp.int32, (rows, 128), 1), HD)
    named = jnp.where(docs == column.astype(jnp.float32), 1.0, 0.0)
    flags = jnp.where(column < 7, 1.0, 0.0)
    return jnp.where(column < 4, named, flags).astype(jnp.bfloat16)


def load_rows(parts):
    return jnp.concatenate([ref[first : first + count, :] for ref, first, count in parts], axis=0)


def scores_of(keys, extras, queries):
    low = lax.broadcasted_iota(jnp.int32, extras.shape, 1) < HD
    scores = []
    for h in range(STEP_HEADS):
        pair = keys[:, h // 2 * 128 : h // 2 * 128 + 128]
        mixed = jnp.where(low, pair, extras) if h % 2 == 0 else jnp.where(low, extras, pair)
        scores.append(jnp.dot(mixed, queries[h], preferred_element_type=jnp.float32))
    return scores


def with_ones(values, h):
    ones = jnp.ones((16, values.shape[1]), jnp.bfloat16)
    return jnp.concatenate([values[h * HD : (h + 1) * HD], ones], axis=0)


def project(x, weight_ref, j):
    columns = weight_ref[:, j * STEP_COLS : (j + 1) * STEP_COLS]
    return jnp.dot(x, columns, preferred_element_type=jnp.float32)


def project_turned(x, weight_ref, j):
    return lax.dot_general(
        weight_ref[j * STEP_COLS : (j + 1) * STEP_COLS, :],
        x,
        (((1,), (1,)), ((), ())),
        preferred_element_type=jnp.float32,
    ).astype(jnp.bfloat16)


def own_kernel(piece, parts, borders_at, *refs):
    row_refs, (wq_ref, wk_ref, wv_ref, queries_ref, state_ref) = refs[:-5], refs[-5:]
    x = load_rows([(row_refs[i], first, count) for i, first, count in parts])
    rows = x.shape[0]
    borders = borders_of(row_refs[borders_at[0]], borders_at[1])
    docs = doc_numbers(borders, places_of(rows, piece, (8, rows), 1))
    row = lax.broadcasted_iota(jnp.int32, (HD, rows), 0)
    differs = jnp.where(docs[0:1, :] == row.astype(jnp.float32), 0.0, -BIG)
    mask_rows = jnp.where(row < 4, differs, 0.0)
    extras = key_extras(borders, rows, piece)
    for j in range(HEADS // STEP_HEADS):
        queries = project(x, wq_ref, j).astype(jnp.bfloat16).astype(jnp.float32)
        queries = (queries * (1.0 / math.sqrt(HD))).T.astype(jnp.bfloat16)
        keys = project(x, wk_ref, j).astype(jnp.bfloat16)
        values = project_turned(x, wv_ref, j)

        def stacked(h, rest):
            own = queries[h * HD : (h + 1) * HD]
            return jnp.concatenate([own, rest] if h % 2 == 0 else [rest, own], axis=0)

        plain = mask_rows.astype(jnp.bfloat16)
        scores = scores_of(keys, extras, [stacked(h, plain) for h in range(STEP_HEADS)])
        tops = [jnp.max(member, axis=0, keepdims=True) for member in scores]
        weights = [
            jnp.exp2((member - top) * LOG2E).astype(jnp.bfloat16)
            for member, top in zip(scores, tops)
        ]
        sums = [
            jnp.dot(with_ones(values, h), weights[h], preferred_element_type=jnp.float32)
            for h in range(STEP_HEADS)
        ]
        for h in range(STEP_HEADS):
            upper = tops[h].astype(jnp.bfloat16).astype(jnp.float32)
            middle = (tops[h] - upper).astype(jnp.bfloat16).astype(jnp.float32)
            lower = tops[h] - upper - middle
            rest = jnp.where(row == 4, -upper, mask_rows)
            rest = jnp.where(row == 5, -middle, rest)
            rest = jnp.where(row == 6, -lower, rest)
            queries_ref[j * STEP_HEADS + h] = stacked(h, rest.astype(jnp.bfloat16))
            state_ref[j * STEP_HEADS + h, : HD + 8, :] = sums[h][: HD + 8]
            state_ref[j * STEP_HEADS + h, HD + 8 :, :] = jnp.zeros((8, rows), jnp.float32)


def fold(piece, sources, queries_ref, wk_ref, wv_ref, state_ref, finish):
    x = jnp.concatenate([load_rows(parts) for parts, _, _ in sources], axis=0)
    extras = jnp.concatenate(
        [
            key_extras(borders_of(ref, first), sum(count for _, _, count in parts), piece)
            for parts, ref, first in sources
        ],
        axis=0,
    )
    largest, excess = [], []
    for j in range(HEADS // STEP_HEADS):
        heads = [j * STEP_HEADS + h for h in range(STEP_HEADS)]
        keys = project(x, wk_ref, j).astype(jnp.bfloat16)
        values = project_turned(x, wv_ref, j)
        scores = scores_of(keys, extras, [queries_ref[head] for head in heads])
        weights = [jnp.exp2(member * LOG2E).astype(jnp.bfloat16) for member in scores]
        sums = [
            state_ref[head, : HD + 8, :]
            + jnp.dot(with_ones(values, h), weights[h], preferred_element_type=jnp.float32)[: HD + 8]
            for h, head in enumerate(heads)
        ]
        for h, head in enumerate(heads):
            finish(head, sums[h], None)
            largest.append(sums[h][HD : HD + 8])
            excess.append(state_ref[head, HD + 8 :, :])
    largest = functools.reduce(jnp.maximum, largest)
    excess = functools.reduce(jnp.maximum, excess)
    usual = jnp.logical_and(largest < LARGEST, excess <= 0.0)

    @pl.when(jnp.min(jnp.where(usual, 1.0, 0.0)) < 0.5)
    def again():
        for j in range(HEADS // STEP_HEADS):
            heads = [j * STEP_HEADS + h for h in range(STEP_HEADS)]
            keys = project(x, wk_ref, j).astype(jnp.bfloat16)
            values = project_turned(x, wv_ref, j)
            scores = scores_of(keys, extras, [queries_ref[head] for head in heads])
            for h, head in enumerate(heads):
                before = state_ref[head, HD + 8 : HD + 9, :]
                top = jnp.maximum(before, jnp.max(scores[h], axis=0, keepdims=True))
                weights = jnp.exp2((scores[h] - top) * LOG2E).astype(jnp.bfloat16)
                added = jnp.dot(with_ones(values, h), weights, preferred_element_type=jnp.float32)
                factor = jnp.exp2((before - top) * LOG2E)
                finish(
                    head,
                    state_ref[head, : HD + 8, :] * factor + added[: HD + 8],
                    jnp.broadcast_to(top, (8, top.shape[1])),
                )


def named_sources(row_refs, layout):
    return [
        ([(row_refs[i], first, count) for i, first, count in parts], row_refs[at], first_border)
        for parts, (at, first_border) in layout
    ]


def chunk_kernel(piece, layout, queries_ref, wk_ref, wv_ref, old_ref, *rest):
    row_refs, state_ref = rest[:-1], rest[-1]

    def finish(head, sums, top):
        state_ref[head, : HD + 8, :] = sums
        state_ref[head, HD + 8 :, :] = jnp.zeros((8, sums.shape[1]), jnp.float32) if top is None else top

    fold(piece, named_sources(row_refs, layout), queries_ref, wk_ref, wv_ref, old_ref, finish)


def last_kernel(groups, piece, layout, queries_ref, wk_ref, wv_ref, old_ref, wo_ref, *rest):
    row_refs = rest[: -2 * groups - 1]
    piece_refs, out_refs = rest[-2 * groups - 1 : -groups - 1], rest[-groups - 1 : -1]
    attended_ref = rest[-1]

    def finish(head, sums, top):
        attended_ref[head * HD : (head + 1) * HD, :] = sums[:HD] / sums[HD : HD + 1]

    fold(piece, named_sources(row_refs, layout), queries_ref, wk_ref, wv_ref, old_ref, finish)
    attended = attended_ref[...].T.astype(jnp.bfloat16)
    mixed = jnp.dot(attended, wo_ref[...], preferred_element_type=jnp.float32)
    for r in range(groups):
        out_refs[r][...] = (
            piece_refs[r][...].astype(jnp.float32) + mixed[r * piece : (r + 1) * piece]
        ).astype(jnp.bfloat16)


def own_call(members, layout, w_query, w_key, w_value, piece, rows):
    parts, borders_at = layout
    return pl.pallas_call(
        functools.partial(own_kernel, piece, parts, borders_at),
        out_shape=[
            jax.ShapeDtypeStruct((HEADS, 2 * HD, rows), jnp.bfloat16),
            jax.ShapeDtypeStruct((HEADS, STATE_ROWS, rows), jnp.float32),
        ],
        in_specs=vmem(len(members) + 3),
        out_specs=vmem(2),
        compiler_params=params(),
        cost_estimate=cost(3.0),
        name="own_rows",
    )(*members, w_query, w_key, w_value)


def chunk_call(queries, w_key, w_value, state, members, layout, piece):
    return pl.pallas_call(
        functools.partial(chunk_kernel, piece, layout),
        out_shape=jax.ShapeDtypeStruct(state.shape, jnp.float32),
        in_specs=vmem(4 + len(members)),
        out_specs=vmem(1)[0],
        compiler_params=params(),
        cost_estimate=cost(3.5),
        name="received_rows",
    )(queries, w_key, w_value, state, *members)


def last_call(queries, w_key, w_value, state, w_out, members, layout, pieces, piece):
    groups, width = len(pieces), w_key.shape[0]
    rows = queries.shape[2]
    return pl.pallas_call(
        functools.partial(last_kernel, groups, piece, layout),
        out_shape=[jax.ShapeDtypeStruct((piece, width), jnp.bfloat16)] * groups,
        in_specs=vmem(5 + len(members) + groups),
        out_specs=vmem(groups),
        scratch_shapes=[pltpu.VMEM((HEADS * HD, rows), jnp.float32)],
        compiler_params=params(),
        cost_estimate=cost(3.0),
        name="last_rows",
    )(queries, w_key, w_value, state, w_out, *members, *pieces)


def arrange_kernel(groups, listing_ref, *refs):
    piece_refs, out_ref = refs[:groups], refs[groups]
    piece = piece_refs[0].shape[0]
    own = lax.axis_index("group")
    for r in range(groups):
        place = piece_of(listing_ref, lax.bitwise_xor(own, jnp.int32(r)), groups)
        out_ref[pl.ds(pl.multiple_of(place * piece, piece), piece), :] = piece_refs[r][...]


def arrange(packing_list, pieces):
    groups, (piece, width) = len(pieces), pieces[0].shape
    return pl.pallas_call(
        functools.partial(arrange_kernel, groups),
        out_shape=jax.ShapeDtypeStruct((groups * piece, width), jnp.bfloat16),
        in_specs=[smem()] + vmem(groups),
        out_specs=vmem(1)[0],
        compiler_params=params(),
        cost_estimate=cost(1.3),
        name="arrange",
    )(packing_list, *pieces)


def exchange(pieces):
    groups = len(pieces)
    return [pieces[0]] + [
        lax.ppermute(pieces[r], "group", [(i, i ^ r) for i in range(groups)])
        for r in range(1, groups)
    ]


def on_device(
    series, recon_mask, mask_token, packing_list, doc_ids, norm_gain, w_query, w_key, w_value, w_out
):
    groups, shards = lax.axis_size("group"), lax.axis_size("ctx")
    rows, width = series.shape
    piece = rows // groups
    ring = list(range(0, shards, 2)) + list(range(shards - 1, 0, -2))
    onward = [(ring[i], ring[(i + 1) % shards]) for i in range(shards)]
    backward = [(there, here) for here, there in onward]

    half = rows // 2
    sent = route(packing_list, series, recon_mask, mask_token, groups)
    w_query, w_key = stage((w_query, w_key), None, sent[0], 2.0)
    pieces = exchange(sent)
    a = norm(pieces[: groups // 2], norm_gain, doc_ids, (w_query,))
    w_value, w_out = stage((w_value, w_out), 0, a, 2.0)
    b = norm(pieces[groups // 2 :], norm_gain, None, (a, w_value))
    own = (a, b)
    own_layout = ([(0, 0, half), (1, 0, half)], (0, half))
    pair_layout = (own_layout, ([(2, 0, half), (3, 0, half)], (2, half)))
    far_layout = (own_layout,)
    queries, state = own_call(own, own_layout, w_query, w_key, w_value, piece, rows)
    before, after = own, own
    for step in range(1, shards // 2):
        before = tuple(lax.ppermute(member, "ctx", onward) for member in before)
        after = tuple(lax.ppermute(member, "ctx", backward) for member in after)
        state = chunk_call(queries, w_key, w_value, state, before + after, pair_layout, piece)
    far = (
        lax.ppermute(before[0], "ctx", onward),
        lax.ppermute(after[1], "ctx", backward),
    )
    done = last_call(queries, w_key, w_value, state, w_out, far, far_layout, pieces, piece)
    return arrange(packing_list, exchange(done))


def solution(mesh):
    in_specs = (
        P(("group", "ctx"), None),
        P(("group", "ctx")),
        P(),
        P(("group", "ctx")),
        P("group", "ctx"),
        P(),
        P(),
        P(),
        P(),
        P(),
    )
    out_specs = P(("group", "ctx"), None)
    return jax.shard_map(
        on_device, mesh=mesh, in_specs=in_specs, out_specs=out_specs, check_vma=False
    )
```

```python
import functools
import math

import jax
import jax.numpy as jnp
from jax import lax
from jax.experimental import pallas as pl
from jax.experimental.pallas import tpu as pltpu
from jax.sharding import PartitionSpec as P

HEADS = 12
HD = 64
STEP_HEADS = 4
STEP_COLS = STEP_HEADS * HD
STATE_ROWS = HD + 16
BIG = 3.3895313892515355e38
LARGEST = 1e30
LOG2E = 1.4426950408889634
COST = 0.05 * 1.1e9
LARGE = 56 * 1024 * 1024
VMEM_LIMIT = 32 * 1024 * 1024


def vmem(count):
    return [pl.BlockSpec(memory_space=pltpu.VMEM)] * count


def hbm(count):
    return [pl.BlockSpec(memory_space=pltpu.HBM)] * count


def anywhere(count):
    return [pl.BlockSpec(memory_space=pl.ANY)] * count


def smem():
    return pl.BlockSpec(memory_space=pltpu.SMEM)


def params(limit=VMEM_LIMIT):
    return pltpu.CompilerParams(vmem_limit_bytes=limit)


def cost(us):
    return pl.CostEstimate(flops=int(us * COST), bytes_accessed=0, transcendentals=0)


def piece_of(listing_ref, group, groups):
    place = jnp.int32(0)
    for k in range(groups):
        place = place + jnp.where(listing_ref[k] == group, jnp.int32(k), jnp.int32(0))
    return place


def route_kernel(
    groups, from_ref, series_ref, mask_ref, token_ref, gain_ref, docs_ref, *rest
):
    out_refs, masked_ref = rest[:groups], rest[groups]
    listing_ref, held_ref, lines_ref, word_ref, scale_ref, numbers_ref, sems = rest[groups + 1 :]
    rows, width = series_ref.shape
    piece = rows // groups
    own = lax.axis_index("group")
    copies = [
        pltpu.make_async_copy(from_ref, listing_ref, sems.at[0]),
        pltpu.make_async_copy(mask_ref, lines_ref, sems.at[1]),
        pltpu.make_async_copy(token_ref, word_ref, sems.at[2]),
        pltpu.make_async_copy(series_ref, held_ref, sems.at[3]),
        pltpu.make_async_copy(gain_ref, scale_ref, sems.at[4]),
        pltpu.make_async_copy(docs_ref, numbers_ref, sems.at[5]),
    ]
    for copy in copies:
        copy.start()
    for copy in copies:
        copy.wait()
    token = word_ref[...].reshape(1, width)
    for part in range(lines_ref.shape[0]):
        line = lines_ref[part : part + 1, :].astype(jnp.float32)
        hidden = jnp.broadcast_to(line, (128, 128)).T > 0.5
        here = slice(part * 128, (part + 1) * 128)
        for lane in range(0, width, 128):
            masked_ref[here, lane : lane + 128] = jnp.where(
                hidden,
                token[:, lane : lane + 128].astype(jnp.float32),
                held_ref[here, lane : lane + 128].astype(jnp.float32),
            ).astype(jnp.bfloat16)
    gain = scale_ref[...].astype(jnp.float32).reshape(1, width)
    for r in range(groups):
        place = piece_of(listing_ref, lax.bitwise_xor(own, jnp.int32(r)), groups)
        widened = masked_ref[pl.ds(pl.multiple_of(place * piece, piece), piece), :].astype(jnp.float32)
        factor = lax.rsqrt(jnp.mean(widened * widened, axis=-1, keepdims=True) + 1e-06)
        out_refs[r][:piece, :] = (widened * factor * gain).astype(jnp.bfloat16)
    row = lax.broadcasted_iota(jnp.int32, (8, width), 0)
    lines = jnp.zeros((8, width), jnp.float32)
    for d in (1, 2, 3):
        below = jnp.sum(jnp.where(numbers_ref[...] < d, 1.0, 0.0), axis=-1, keepdims=True)
        lines = jnp.where(row == d, below, lines)
    out_refs[0][piece:, :] = lines.astype(jnp.bfloat16)


def route(packing_list, series, recon_mask, mask_token, norm_gain, doc_ids, groups):
    rows, width = series.shape
    piece = rows // groups
    *pieces, masked = pl.pallas_call(
        functools.partial(route_kernel, groups),
        out_shape=[
            jax.ShapeDtypeStruct((piece + 8 if r == 0 else piece, width), jnp.bfloat16)
            for r in range(groups)
        ]
        + [jax.ShapeDtypeStruct((rows, width), jnp.bfloat16)],
        in_specs=anywhere(6),
        out_specs=vmem(groups + 1),
        scratch_shapes=[
            pltpu.SMEM((groups,), jnp.int32),
            pltpu.VMEM((rows, width), jnp.bfloat16),
            pltpu.VMEM((rows // 128, 128), jnp.int32),
            pltpu.VMEM((width,), jnp.bfloat16),
            pltpu.VMEM((width,), jnp.bfloat16),
            pltpu.VMEM(doc_ids.shape, jnp.int32),
            pltpu.SemaphoreType.DMA((6,)),
        ],
        compiler_params=params(LARGE),
        cost_estimate=cost(100.0),
        name="route",
    )(
        packing_list,
        series,
        recon_mask.reshape(rows // 128, 128),
        mask_token,
        norm_gain,
        doc_ids,
    )
    return pieces, masked


def stage_kernel(count, turned, *refs):
    from_refs, to_refs = refs[:count], refs[count + 1 : 2 * count + 1]
    scratch, sems = refs[2 * count + 1 : -1], refs[-1]
    copies = []
    for i in range(count):
        target = scratch[0] if i == turned else to_refs[i]
        copies.append(pltpu.make_async_copy(from_refs[i], target, sems.at[i]))
    for copy in copies:
        copy.start()
    for copy in copies:
        copy.wait()
    if turned is not None:
        width = to_refs[turned].shape[0]
        for lane in range(0, width, 256):
            to_refs[turned][lane : lane + 256, :] = (
                scratch[0][:, lane : lane + 256].astype(jnp.float32).T.astype(jnp.bfloat16)
            )


def stage(weights, turned, behind, us):
    count = len(weights)
    scratch = [pltpu.VMEM(weights[turned].shape, jnp.bfloat16)] if turned is not None else []
    return pl.pallas_call(
        functools.partial(stage_kernel, count, turned),
        out_shape=[jax.ShapeDtypeStruct(member.shape, member.dtype) for member in weights],
        in_specs=hbm(count) + anywhere(1),
        out_specs=vmem(count),
        scratch_shapes=scratch + [pltpu.SemaphoreType.DMA((count,))],
        compiler_params=params(),
        cost_estimate=cost(us),
        name="stage",
    )(*weights, behind)


def join_kernel(spans, *refs):
    out_ref, at = refs[-1], 0
    for i, first, count in spans:
        out_ref[at : at + count, :] = refs[i][first : first + count, :]
        at += count


def join(members, spans, behind=()):
    rows, width = sum(count for _, _, count in spans), members[0].shape[1]
    return pl.pallas_call(
        functools.partial(join_kernel, spans),
        out_shape=jax.ShapeDtypeStruct((rows, width), jnp.bfloat16),
        in_specs=vmem(len(members)) + anywhere(len(behind)),
        out_specs=vmem(1)[0],
        compiler_params=params(),
        cost_estimate=cost(0.2),
        name="join",
    )(*members, *behind)


def borders_of(ref, first):
    return ref[first : first + 8, :].astype(jnp.float32)


def places_of(count, piece, shape, axis):
    own = lax.axis_index("group")
    held = lax.broadcasted_iota(jnp.int32, shape, axis)
    source = lax.bitwise_xor(held // piece, own)
    return (source * piece + held % piece).astype(jnp.float32)


def doc_numbers(borders, place):
    docs = jnp.zeros(place.shape, jnp.float32)
    for d in (1, 2, 3):
        docs = docs + jnp.where(place >= borders[d : d + 1, : place.shape[1]], 1.0, 0.0)
    return docs


def key_extras(borders, rows, piece):
    docs = doc_numbers(borders, places_of(rows, piece, (rows, 128), 0))
    column = lax.rem(lax.broadcasted_iota(jnp.int32, (rows, 128), 1), HD)
    named = jnp.where(docs == column.astype(jnp.float32), 1.0, 0.0)
    flags = jnp.where(column < 7, 1.0, 0.0)
    return jnp.where(column < 4, named, flags).astype(jnp.bfloat16)


def load_rows(parts):
    return jnp.concatenate([ref[first : first + count, :] for ref, first, count in parts], axis=0)


def scores_of(keys, extras, queries):
    low = lax.broadcasted_iota(jnp.int32, extras.shape, 1) < HD
    scores = []
    for h in range(STEP_HEADS):
        pair = keys[:, h // 2 * 128 : h // 2 * 128 + 128]
        mixed = jnp.where(low, pair, extras) if h % 2 == 0 else jnp.where(low, extras, pair)
        scores.append(jnp.dot(mixed, queries[h], preferred_element_type=jnp.float32))
    return scores


def with_ones(values, h):
    ones = jnp.ones((16, values.shape[1]), jnp.bfloat16)
    return jnp.concatenate([values[h * HD : (h + 1) * HD], ones], axis=0)


def project(x, weight_ref, j):
    columns = weight_ref[:, j * STEP_COLS : (j + 1) * STEP_COLS]
    return jnp.dot(x, columns, preferred_element_type=jnp.float32)


def project_turned(x, weight_ref, j):
    return lax.dot_general(
        weight_ref[j * STEP_COLS : (j + 1) * STEP_COLS, :],
        x,
        (((1,), (1,)), ((), ())),
        preferred_element_type=jnp.float32,
    ).astype(jnp.bfloat16)


def own_kernel(piece, parts, borders_at, *refs):
    row_refs, (wq_ref, wk_ref, wv_ref, queries_ref, state_ref) = refs[:-5], refs[-5:]
    x = load_rows([(row_refs[i], first, count) for i, first, count in parts])
    rows = x.shape[0]
    borders = borders_of(row_refs[borders_at[0]], borders_at[1])
    docs = doc_numbers(borders, places_of(rows, piece, (8, rows), 1))
    row = lax.broadcasted_iota(jnp.int32, (HD, rows), 0)
    differs = jnp.where(docs[0:1, :] == row.astype(jnp.float32), 0.0, -BIG)
    mask_rows = jnp.where(row < 4, differs, 0.0)
    extras = key_extras(borders, rows, piece)
    for j in range(HEADS // STEP_HEADS):
        queries = project(x, wq_ref, j).astype(jnp.bfloat16).astype(jnp.float32)
        queries = (queries * (1.0 / math.sqrt(HD))).T.astype(jnp.bfloat16)
        keys = project(x, wk_ref, j).astype(jnp.bfloat16)
        values = project_turned(x, wv_ref, j)

        def stacked(h, rest):
            own = queries[h * HD : (h + 1) * HD]
            return jnp.concatenate([own, rest] if h % 2 == 0 else [rest, own], axis=0)

        plain = mask_rows.astype(jnp.bfloat16)
        scores = scores_of(keys, extras, [stacked(h, plain) for h in range(STEP_HEADS)])
        tops = [jnp.max(member, axis=0, keepdims=True) for member in scores]
        weights = [
            jnp.exp2((member - top) * LOG2E).astype(jnp.bfloat16)
            for member, top in zip(scores, tops)
        ]
        sums = [
            jnp.dot(with_ones(values, h), weights[h], preferred_element_type=jnp.float32)
            for h in range(STEP_HEADS)
        ]
        for h in range(STEP_HEADS):
            upper = tops[h].astype(jnp.bfloat16).astype(jnp.float32)
            middle = (tops[h] - upper).astype(jnp.bfloat16).astype(jnp.float32)
            lower = tops[h] - upper - middle
            rest = jnp.where(row == 4, -upper, mask_rows)
            rest = jnp.where(row == 5, -middle, rest)
            rest = jnp.where(row == 6, -lower, rest)
            queries_ref[j * STEP_HEADS + h] = stacked(h, rest.astype(jnp.bfloat16))
            state_ref[j * STEP_HEADS + h, : HD + 8, :] = sums[h][: HD + 8]
            state_ref[j * STEP_HEADS + h, HD + 8 :, :] = jnp.zeros((8, rows), jnp.float32)


def fold(piece, sources, queries_ref, wk_ref, wv_ref, state_ref, finish):
    x = jnp.concatenate([load_rows(parts) for parts, _, _ in sources], axis=0)
    extras = jnp.concatenate(
        [
            key_extras(borders_of(ref, first), sum(count for _, _, count in parts), piece)
            for parts, ref, first in sources
        ],
        axis=0,
    )
    largest, excess = [], []
    for j in range(HEADS // STEP_HEADS):
        heads = [j * STEP_HEADS + h for h in range(STEP_HEADS)]
        keys = project(x, wk_ref, j).astype(jnp.bfloat16)
        values = project_turned(x, wv_ref, j)
        scores = scores_of(keys, extras, [queries_ref[head] for head in heads])
        weights = [jnp.exp2(member * LOG2E).astype(jnp.bfloat16) for member in scores]
        sums = [
            state_ref[head, : HD + 8, :]
            + jnp.dot(with_ones(values, h), weights[h], preferred_element_type=jnp.float32)[: HD + 8]
            for h, head in enumerate(heads)
        ]
        for h, head in enumerate(heads):
            finish(head, sums[h], None)
            largest.append(sums[h][HD : HD + 8])
            excess.append(state_ref[head, HD + 8 :, :])
    largest = functools.reduce(jnp.maximum, largest)
    excess = functools.reduce(jnp.maximum, excess)
    usual = jnp.logical_and(largest < LARGEST, excess <= 0.0)

    @pl.when(jnp.min(jnp.where(usual, 1.0, 0.0)) < 0.5)
    def again():
        for j in range(HEADS // STEP_HEADS):
            heads = [j * STEP_HEADS + h for h in range(STEP_HEADS)]
            keys = project(x, wk_ref, j).astype(jnp.bfloat16)
            values = project_turned(x, wv_ref, j)
            scores = scores_of(keys, extras, [queries_ref[head] for head in heads])
            for h, head in enumerate(heads):
                before = state_ref[head, HD + 8 : HD + 9, :]
                top = jnp.maximum(before, jnp.max(scores[h], axis=0, keepdims=True))
                weights = jnp.exp2((scores[h] - top) * LOG2E).astype(jnp.bfloat16)
                added = jnp.dot(with_ones(values, h), weights, preferred_element_type=jnp.float32)
                factor = jnp.exp2((before - top) * LOG2E)
                finish(
                    head,
                    state_ref[head, : HD + 8, :] * factor + added[: HD + 8],
                    jnp.broadcast_to(top, (8, top.shape[1])),
                )


def named_sources(row_refs, layout):
    return [
        ([(row_refs[i], first, count) for i, first, count in parts], row_refs[at], first_border)
        for parts, (at, first_border) in layout
    ]


def chunk_kernel(piece, layout, queries_ref, wk_ref, wv_ref, old_ref, *rest):
    row_refs, state_ref = rest[:-1], rest[-1]

    def finish(head, sums, top):
        state_ref[head, : HD + 8, :] = sums
        state_ref[head, HD + 8 :, :] = jnp.zeros((8, sums.shape[1]), jnp.float32) if top is None else top

    fold(piece, named_sources(row_refs, layout), queries_ref, wk_ref, wv_ref, old_ref, finish)


def last_kernel(groups, piece, layout, queries_ref, wk_ref, wv_ref, old_ref, wo_ref, *rest):
    row_refs, out_refs = rest[: -groups - 1], rest[-groups - 1 : -1]
    attended_ref = rest[-1]

    def finish(head, sums, top):
        attended_ref[head * HD : (head + 1) * HD, :] = sums[:HD] / sums[HD : HD + 1]

    fold(piece, named_sources(row_refs, layout), queries_ref, wk_ref, wv_ref, old_ref, finish)
    attended = attended_ref[...].T.astype(jnp.bfloat16)
    mixed = jnp.dot(attended, wo_ref[...], preferred_element_type=jnp.float32)
    for r in range(groups):
        out_refs[r][...] = mixed[r * piece : (r + 1) * piece].astype(jnp.bfloat16)


def own_call(members, layout, w_query, w_key, w_value, piece, rows):
    parts, borders_at = layout
    return pl.pallas_call(
        functools.partial(own_kernel, piece, parts, borders_at),
        out_shape=[
            jax.ShapeDtypeStruct((HEADS, 2 * HD, rows), jnp.bfloat16),
            jax.ShapeDtypeStruct((HEADS, STATE_ROWS, rows), jnp.float32),
        ],
        in_specs=vmem(len(members) + 3),
        out_specs=vmem(2),
        compiler_params=params(),
        cost_estimate=cost(3.0),
        name="own_rows",
    )(*members, w_query, w_key, w_value)


def chunk_call(queries, w_key, w_value, state, members, layout, piece):
    return pl.pallas_call(
        functools.partial(chunk_kernel, piece, layout),
        out_shape=jax.ShapeDtypeStruct(state.shape, jnp.float32),
        in_specs=vmem(4 + len(members)),
        out_specs=vmem(1)[0],
        compiler_params=params(),
        cost_estimate=cost(3.5),
        name="received_rows",
    )(queries, w_key, w_value, state, *members)


def last_call(queries, w_key, w_value, state, w_out, members, layout, groups, piece):
    width = w_key.shape[0]
    rows = queries.shape[2]
    return pl.pallas_call(
        functools.partial(last_kernel, groups, piece, layout),
        out_shape=[jax.ShapeDtypeStruct((piece, width), jnp.bfloat16)] * groups,
        in_specs=vmem(5 + len(members)),
        out_specs=vmem(groups),
        scratch_shapes=[pltpu.VMEM((HEADS * HD, rows), jnp.float32)],
        compiler_params=params(),
        cost_estimate=cost(3.0),
        name="last_rows",
    )(queries, w_key, w_value, state, w_out, *members)


def arrange_kernel(groups, listing_ref, masked_ref, *refs):
    piece_refs, out_ref = refs[:groups], refs[groups]
    piece = piece_refs[0].shape[0]
    own = lax.axis_index("group")
    for r in range(groups):
        place = piece_of(listing_ref, lax.bitwise_xor(own, jnp.int32(r)), groups)
        here = pl.ds(pl.multiple_of(place * piece, piece), piece)
        out_ref[here, :] = (
            masked_ref[here, :].astype(jnp.float32) + piece_refs[r][...].astype(jnp.float32)
        ).astype(jnp.bfloat16)


def arrange(packing_list, masked, pieces):
    groups, (piece, width) = len(pieces), pieces[0].shape
    return pl.pallas_call(
        functools.partial(arrange_kernel, groups),
        out_shape=jax.ShapeDtypeStruct((groups * piece, width), jnp.bfloat16),
        in_specs=[smem()] + vmem(groups + 1),
        out_specs=vmem(1)[0],
        compiler_params=params(),
        cost_estimate=cost(1.3),
        name="arrange",
    )(packing_list, masked, *pieces)


def hold_kernel(*refs):
    pass


def hold(members, *behind):
    count = len(members)
    return tuple(
        pl.pallas_call(
            hold_kernel,
            out_shape=[jax.ShapeDtypeStruct(member.shape, member.dtype) for member in members],
            in_specs=anywhere(count + len(behind)),
            out_specs=anywhere(count),
            input_output_aliases={i: i for i in range(count)},
            compiler_params=params(),
            cost_estimate=cost(0.1),
            name="hold",
        )(*members, *behind)
    )


def exchange(pieces):
    groups = len(pieces)
    return [pieces[0]] + [
        lax.ppermute(pieces[r], "group", [(i, i ^ r) for i in range(groups)])
        for r in range(1, groups)
    ]


def on_device(
    series, recon_mask, mask_token, packing_list, doc_ids, norm_gain, w_query, w_key, w_value, w_out
):
    groups, shards = lax.axis_size("group"), lax.axis_size("ctx")
    rows, width = series.shape
    piece = rows // groups
    ring = list(range(0, shards, 2)) + list(range(shards - 1, 0, -2))
    onward = [(ring[i], ring[(i + 1) % shards]) for i in range(shards)]
    backward = [(there, here) for here, there in onward]

    half = rows // 2
    sent, masked = route(
        packing_list, series, recon_mask, mask_token, norm_gain, doc_ids, groups
    )
    w_query, w_key, w_value = stage((w_query, w_key, w_value), 2, sent[0], 0.01)
    pieces = exchange(sent)
    low = groups // 2
    spans = [(r, 0, piece) for r in range(low)]
    a = join(pieces[:low], spans + [(0, piece, 8)])
    b = join(pieces[low:], spans, (a, w_value))

    def onto(member):
        return lax.ppermute(member, "ctx", onward)

    def back(member):
        return lax.ppermute(member, "ctx", backward)

    own_layout = ([(0, 0, half), (1, 0, half)], (0, half))
    pair_layout = (own_layout, ([(2, 0, half), (3, 0, half)], (2, half)))
    far_layout = (own_layout,)
    queries, state = own_call((a, b), own_layout, w_query, w_key, w_value, piece, rows)
    a_before, a_after, b_before, b_after = a, a, b, b
    for step in range(1, shards // 2):
        a_before, a_after = hold((onto(a_before), back(a_after)))
        b_before, b_after = hold((onto(b_before), back(b_after)), state)
        received = (a_before, b_before, a_after, b_after)
        state = chunk_call(queries, w_key, w_value, state, received, pair_layout, piece)
    far = (onto(a_before), back(b_after))
    done = last_call(queries, w_key, w_value, state, w_out, far, far_layout, groups, piece)
    return arrange(packing_list, masked, exchange(done))


def solution(mesh):
    in_specs = (
        P(("group", "ctx"), None),
        P(("group", "ctx")),
        P(),
        P(("group", "ctx")),
        P("group", "ctx"),
        P(),
        P(),
        P(),
        P(),
        P(),
    )
    out_specs = P(("group", "ctx"), None)
    return jax.shard_map(
        on_device, mesh=mesh, in_specs=in_specs, out_specs=out_specs, check_vma=False
    )
```

```python
import functools
import math

import jax
import jax.numpy as jnp
from jax import lax
from jax.experimental import pallas as pl
from jax.experimental.pallas import tpu as pltpu
from jax.sharding import PartitionSpec as P

HEADS = 12
AH = 0.1
BH = 0.1
HD = 64
STEP_HEADS = 4
STEP_COLS = STEP_HEADS * HD
STATE_ROWS = HD + 16
BIG = 3.3895313892515355e38
LARGEST = 1e30
LOG2E = 1.4426950408889634
COST = 0.05 * 1.1e9
LARGE = 56 * 1024 * 1024
VMEM_LIMIT = 32 * 1024 * 1024


def vmem(count):
    return [pl.BlockSpec(memory_space=pltpu.VMEM)] * count


def hbm(count):
    return [pl.BlockSpec(memory_space=pltpu.HBM)] * count


def anywhere(count):
    return [pl.BlockSpec(memory_space=pl.ANY)] * count


def smem():
    return pl.BlockSpec(memory_space=pltpu.SMEM)


def params(limit=VMEM_LIMIT):
    return pltpu.CompilerParams(vmem_limit_bytes=limit)


def cost(us):
    return pl.CostEstimate(flops=int(us * COST), bytes_accessed=0, transcendentals=0)


def piece_of(listing_ref, group, groups):
    place = jnp.int32(0)
    for k in range(groups):
        place = place + jnp.where(listing_ref[k] == group, jnp.int32(k), jnp.int32(0))
    return place


def route_kernel(
    groups, from_ref, series_ref, mask_ref, token_ref, gain_ref, docs_ref, *rest
):
    out_refs, masked_ref = rest[:groups], rest[groups]
    listing_ref, held_ref, lines_ref, word_ref, scale_ref, numbers_ref, sems = rest[groups + 1 :]
    rows, width = series_ref.shape
    piece = rows // groups
    own = lax.axis_index("group")
    copies = [
        pltpu.make_async_copy(from_ref, listing_ref, sems.at[0]),
        pltpu.make_async_copy(mask_ref, lines_ref, sems.at[1]),
        pltpu.make_async_copy(token_ref, word_ref, sems.at[2]),
        pltpu.make_async_copy(series_ref, held_ref, sems.at[3]),
        pltpu.make_async_copy(gain_ref, scale_ref, sems.at[4]),
        pltpu.make_async_copy(docs_ref, numbers_ref, sems.at[5]),
    ]
    for copy in copies:
        copy.start()
    for copy in copies:
        copy.wait()
    token = word_ref[...].reshape(1, width)
    for part in range(lines_ref.shape[0]):
        line = lines_ref[part : part + 1, :].astype(jnp.float32)
        hidden = jnp.broadcast_to(line, (128, 128)).T > 0.5
        here = slice(part * 128, (part + 1) * 128)
        for lane in range(0, width, 128):
            masked_ref[here, lane : lane + 128] = jnp.where(
                hidden,
                token[:, lane : lane + 128].astype(jnp.float32),
                held_ref[here, lane : lane + 128].astype(jnp.float32),
            ).astype(jnp.bfloat16)
    gain = scale_ref[...].astype(jnp.float32).reshape(1, width)
    for r in range(groups):
        place = piece_of(listing_ref, lax.bitwise_xor(own, jnp.int32(r)), groups)
        widened = masked_ref[pl.ds(pl.multiple_of(place * piece, piece), piece), :].astype(jnp.float32)
        factor = lax.rsqrt(jnp.mean(widened * widened, axis=-1, keepdims=True) + 1e-06)
        out_refs[r][:piece, :] = (widened * factor * gain).astype(jnp.bfloat16)
    row = lax.broadcasted_iota(jnp.int32, (8, width), 0)
    lines = jnp.zeros((8, width), jnp.float32)
    for d in (1, 2, 3):
        below = jnp.sum(jnp.where(numbers_ref[...] < d, 1.0, 0.0), axis=-1, keepdims=True)
        lines = jnp.where(row == d, below, lines)
    out_refs[0][piece:, :] = lines.astype(jnp.bfloat16)


def route(packing_list, series, recon_mask, mask_token, norm_gain, doc_ids, groups):
    rows, width = series.shape
    piece = rows // groups
    *pieces, masked = pl.pallas_call(
        functools.partial(route_kernel, groups),
        out_shape=[
            jax.ShapeDtypeStruct((piece + 8 if r == 0 else piece, width), jnp.bfloat16)
            for r in range(groups)
        ]
        + [jax.ShapeDtypeStruct((rows, width), jnp.bfloat16)],
        in_specs=anywhere(6),
        out_specs=vmem(groups + 1),
        scratch_shapes=[
            pltpu.SMEM((groups,), jnp.int32),
            pltpu.VMEM((rows, width), jnp.bfloat16),
            pltpu.VMEM((rows // 128, 128), jnp.int32),
            pltpu.VMEM((width,), jnp.bfloat16),
            pltpu.VMEM((width,), jnp.bfloat16),
            pltpu.VMEM(doc_ids.shape, jnp.int32),
            pltpu.SemaphoreType.DMA((6,)),
        ],
        compiler_params=params(LARGE),
        cost_estimate=cost(100.0),
        name="route",
    )(
        packing_list,
        series,
        recon_mask.reshape(rows // 128, 128),
        mask_token,
        norm_gain,
        doc_ids,
    )
    return pieces, masked


def stage_kernel(count, turned, *refs):
    from_refs, to_refs = refs[:count], refs[count + 1 : 2 * count + 1]
    scratch, sems = refs[2 * count + 1 : -1], refs[-1]
    copies = []
    for i in range(count):
        target = scratch[0] if i == turned else to_refs[i]
        copies.append(pltpu.make_async_copy(from_refs[i], target, sems.at[i]))
    for copy in copies:
        copy.start()
    for copy in copies:
        copy.wait()
    if turned is not None:
        width = to_refs[turned].shape[0]
        for lane in range(0, width, 256):
            to_refs[turned][lane : lane + 256, :] = (
                scratch[0][:, lane : lane + 256].astype(jnp.float32).T.astype(jnp.bfloat16)
            )


def stage(weights, turned, behind, us):
    count = len(weights)
    scratch = [pltpu.VMEM(weights[turned].shape, jnp.bfloat16)] if turned is not None else []
    return pl.pallas_call(
        functools.partial(stage_kernel, count, turned),
        out_shape=[jax.ShapeDtypeStruct(member.shape, member.dtype) for member in weights],
        in_specs=hbm(count) + anywhere(1),
        out_specs=vmem(count),
        scratch_shapes=scratch + [pltpu.SemaphoreType.DMA((count,))],
        compiler_params=params(),
        cost_estimate=cost(us),
        name="stage",
    )(*weights, behind)


def join_kernel(spans, *refs):
    out_ref, at = refs[-1], 0
    for i, first, count in spans:
        out_ref[at : at + count, :] = refs[i][first : first + count, :]
        at += count


def join(members, spans, behind=()):
    rows, width = sum(count for _, _, count in spans), members[0].shape[1]
    return pl.pallas_call(
        functools.partial(join_kernel, spans),
        out_shape=jax.ShapeDtypeStruct((rows, width), jnp.bfloat16),
        in_specs=vmem(len(members)) + anywhere(len(behind)),
        out_specs=vmem(1)[0],
        compiler_params=params(),
        cost_estimate=cost(0.2),
        name="join",
    )(*members, *behind)


def borders_of(ref, first):
    return ref[first : first + 8, :].astype(jnp.float32)


def places_of(count, piece, shape, axis):
    own = lax.axis_index("group")
    held = lax.broadcasted_iota(jnp.int32, shape, axis)
    source = lax.bitwise_xor(held // piece, own)
    return (source * piece + held % piece).astype(jnp.float32)


def doc_numbers(borders, place):
    docs = jnp.zeros(place.shape, jnp.float32)
    for d in (1, 2, 3):
        docs = docs + jnp.where(place >= borders[d : d + 1, : place.shape[1]], 1.0, 0.0)
    return docs


def key_extras(borders, rows, piece):
    docs = doc_numbers(borders, places_of(rows, piece, (rows, 128), 0))
    column = lax.rem(lax.broadcasted_iota(jnp.int32, (rows, 128), 1), HD)
    named = jnp.where(docs == column.astype(jnp.float32), 1.0, 0.0)
    flags = jnp.where(column < 7, 1.0, 0.0)
    return jnp.where(column < 4, named, flags).astype(jnp.bfloat16)


def load_rows(parts):
    return jnp.concatenate([ref[first : first + count, :] for ref, first, count in parts], axis=0)


def scores_of(keys, extras, queries):
    low = lax.broadcasted_iota(jnp.int32, extras.shape, 1) < HD
    scores = []
    for h in range(STEP_HEADS):
        pair = keys[:, h // 2 * 128 : h // 2 * 128 + 128]
        mixed = jnp.where(low, pair, extras) if h % 2 == 0 else jnp.where(low, extras, pair)
        scores.append(jnp.dot(mixed, queries[h], preferred_element_type=jnp.float32))
    return scores


def with_ones(values, h):
    ones = jnp.ones((16, values.shape[1]), jnp.bfloat16)
    return jnp.concatenate([values[h * HD : (h + 1) * HD], ones], axis=0)


def project(x, weight_ref, j):
    columns = weight_ref[:, j * STEP_COLS : (j + 1) * STEP_COLS]
    return jnp.dot(x, columns, preferred_element_type=jnp.float32)


def project_turned(x, weight_ref, j):
    return lax.dot_general(
        weight_ref[j * STEP_COLS : (j + 1) * STEP_COLS, :],
        x,
        (((1,), (1,)), ((), ())),
        preferred_element_type=jnp.float32,
    ).astype(jnp.bfloat16)


def own_kernel(piece, parts, borders_at, *refs):
    row_refs, (wq_ref, wk_ref, wv_ref, queries_ref, state_ref) = refs[:-5], refs[-5:]
    x = load_rows([(row_refs[i], first, count) for i, first, count in parts])
    rows = x.shape[0]
    borders = borders_of(row_refs[borders_at[0]], borders_at[1])
    docs = doc_numbers(borders, places_of(rows, piece, (8, rows), 1))
    row = lax.broadcasted_iota(jnp.int32, (HD, rows), 0)
    differs = jnp.where(docs[0:1, :] == row.astype(jnp.float32), 0.0, -BIG)
    mask_rows = jnp.where(row < 4, differs, 0.0)
    extras = key_extras(borders, rows, piece)
    for j in range(HEADS // STEP_HEADS):
        queries = project(x, wq_ref, j).astype(jnp.bfloat16).astype(jnp.float32)
        queries = (queries * (1.0 / math.sqrt(HD))).T.astype(jnp.bfloat16)
        keys = project(x, wk_ref, j).astype(jnp.bfloat16)
        values = project_turned(x, wv_ref, j)

        def stacked(h, rest):
            own = queries[h * HD : (h + 1) * HD]
            return jnp.concatenate([own, rest] if h % 2 == 0 else [rest, own], axis=0)

        plain = mask_rows.astype(jnp.bfloat16)
        scores = scores_of(keys, extras, [stacked(h, plain) for h in range(STEP_HEADS)])
        tops = [jnp.max(member, axis=0, keepdims=True) for member in scores]
        weights = [
            jnp.exp2((member - top) * LOG2E).astype(jnp.bfloat16)
            for member, top in zip(scores, tops)
        ]
        sums = [
            jnp.dot(with_ones(values, h), weights[h], preferred_element_type=jnp.float32)
            for h in range(STEP_HEADS)
        ]
        for h in range(STEP_HEADS):
            upper = tops[h].astype(jnp.bfloat16).astype(jnp.float32)
            middle = (tops[h] - upper).astype(jnp.bfloat16).astype(jnp.float32)
            lower = tops[h] - upper - middle
            rest = jnp.where(row == 4, -upper, mask_rows)
            rest = jnp.where(row == 5, -middle, rest)
            rest = jnp.where(row == 6, -lower, rest)
            queries_ref[j * STEP_HEADS + h] = stacked(h, rest.astype(jnp.bfloat16))
            state_ref[j * STEP_HEADS + h, : HD + 8, :] = sums[h][: HD + 8]
            state_ref[j * STEP_HEADS + h, HD + 8 :, :] = jnp.zeros((8, rows), jnp.float32)


def fold(piece, sources, queries_ref, wk_ref, wv_ref, state_ref, finish):
    x = jnp.concatenate([load_rows(parts) for parts, _, _ in sources], axis=0)
    extras = jnp.concatenate(
        [
            key_extras(borders_of(ref, first), sum(count for _, _, count in parts), piece)
            for parts, ref, first in sources
        ],
        axis=0,
    )
    largest, excess = [], []
    for j in range(HEADS // STEP_HEADS):
        heads = [j * STEP_HEADS + h for h in range(STEP_HEADS)]
        keys = project(x, wk_ref, j).astype(jnp.bfloat16)
        values = project_turned(x, wv_ref, j)
        scores = scores_of(keys, extras, [queries_ref[head] for head in heads])
        weights = [jnp.exp2(member * LOG2E).astype(jnp.bfloat16) for member in scores]
        sums = [
            state_ref[head, : HD + 8, :]
            + jnp.dot(with_ones(values, h), weights[h], preferred_element_type=jnp.float32)[: HD + 8]
            for h, head in enumerate(heads)
        ]
        for h, head in enumerate(heads):
            finish(head, sums[h], None)
            largest.append(sums[h][HD : HD + 8])
            excess.append(state_ref[head, HD + 8 :, :])
    largest = functools.reduce(jnp.maximum, largest)
    excess = functools.reduce(jnp.maximum, excess)
    usual = jnp.logical_and(largest < LARGEST, excess <= 0.0)

    @pl.when(jnp.min(jnp.where(usual, 1.0, 0.0)) < 0.5)
    def again():
        for j in range(HEADS // STEP_HEADS):
            heads = [j * STEP_HEADS + h for h in range(STEP_HEADS)]
            keys = project(x, wk_ref, j).astype(jnp.bfloat16)
            values = project_turned(x, wv_ref, j)
            scores = scores_of(keys, extras, [queries_ref[head] for head in heads])
            for h, head in enumerate(heads):
                before = state_ref[head, HD + 8 : HD + 9, :]
                top = jnp.maximum(before, jnp.max(scores[h], axis=0, keepdims=True))
                weights = jnp.exp2((scores[h] - top) * LOG2E).astype(jnp.bfloat16)
                added = jnp.dot(with_ones(values, h), weights, preferred_element_type=jnp.float32)
                factor = jnp.exp2((before - top) * LOG2E)
                finish(
                    head,
                    state_ref[head, : HD + 8, :] * factor + added[: HD + 8],
                    jnp.broadcast_to(top, (8, top.shape[1])),
                )


def named_sources(row_refs, layout):
    return [
        ([(row_refs[i], first, count) for i, first, count in parts], row_refs[at], first_border)
        for parts, (at, first_border) in layout
    ]


def chunk_kernel(piece, layout, queries_ref, wk_ref, wv_ref, old_ref, *rest):
    row_refs, state_ref = rest[:-1], rest[-1]

    def finish(head, sums, top):
        state_ref[head, : HD + 8, :] = sums
        state_ref[head, HD + 8 :, :] = jnp.zeros((8, sums.shape[1]), jnp.float32) if top is None else top

    fold(piece, named_sources(row_refs, layout), queries_ref, wk_ref, wv_ref, old_ref, finish)


def last_kernel(groups, piece, layout, queries_ref, wk_ref, wv_ref, old_ref, wo_ref, *rest):
    row_refs, out_refs = rest[: -groups - 1], rest[-groups - 1 : -1]
    attended_ref = rest[-1]

    def finish(head, sums, top):
        attended_ref[head * HD : (head + 1) * HD, :] = sums[:HD] / sums[HD : HD + 1]

    fold(piece, named_sources(row_refs, layout), queries_ref, wk_ref, wv_ref, old_ref, finish)
    attended = attended_ref[...].T.astype(jnp.bfloat16)
    mixed = jnp.dot(attended, wo_ref[...], preferred_element_type=jnp.float32)
    for r in range(groups):
        out_refs[r][...] = mixed[r * piece : (r + 1) * piece].astype(jnp.bfloat16)


def own_call(members, layout, w_query, w_key, w_value, piece, rows):
    parts, borders_at = layout
    return pl.pallas_call(
        functools.partial(own_kernel, piece, parts, borders_at),
        out_shape=[
            jax.ShapeDtypeStruct((HEADS, 2 * HD, rows), jnp.bfloat16),
            jax.ShapeDtypeStruct((HEADS, STATE_ROWS, rows), jnp.float32),
        ],
        in_specs=vmem(len(members) + 3),
        out_specs=vmem(2),
        compiler_params=params(),
        cost_estimate=cost(3.0),
        name="own_rows",
    )(*members, w_query, w_key, w_value)


def chunk_call(queries, w_key, w_value, state, members, layout, piece):
    return pl.pallas_call(
        functools.partial(chunk_kernel, piece, layout),
        out_shape=jax.ShapeDtypeStruct(state.shape, jnp.float32),
        in_specs=vmem(4 + len(members)),
        out_specs=vmem(1)[0],
        compiler_params=params(),
        cost_estimate=cost(3.5),
        name="received_rows",
    )(queries, w_key, w_value, state, *members)


def last_call(queries, w_key, w_value, state, w_out, members, layout, groups, piece):
    width = w_key.shape[0]
    rows = queries.shape[2]
    return pl.pallas_call(
        functools.partial(last_kernel, groups, piece, layout),
        out_shape=[jax.ShapeDtypeStruct((piece, width), jnp.bfloat16)] * groups,
        in_specs=vmem(5 + len(members)),
        out_specs=vmem(groups),
        scratch_shapes=[pltpu.VMEM((HEADS * HD, rows), jnp.float32)],
        compiler_params=params(),
        cost_estimate=cost(3.0),
        name="last_rows",
    )(queries, w_key, w_value, state, w_out, *members)


def arrange_kernel(groups, listing_ref, masked_ref, *refs):
    piece_refs, out_ref, sums_ref, sems = refs[:groups], refs[-3], refs[-2], refs[-1]
    piece = piece_refs[0].shape[0]
    own = lax.axis_index("group")
    copies = []
    for k in range(groups):
        group = listing_ref[0:1, k : k + 1]
        here = slice(k * piece, (k + 1) * piece)
        back = piece_refs[0][...].astype(jnp.float32)
        for r in range(1, groups):
            mine = group == lax.bitwise_xor(own, jnp.int32(r))
            back = jnp.where(mine, piece_refs[r][...].astype(jnp.float32), back)
        sums_ref[here, :] = (masked_ref[here, :].astype(jnp.float32) + back).astype(jnp.bfloat16)
        copies.append(pltpu.make_async_copy(sums_ref.at[here, :], out_ref.at[here, :], sems.at[k]))
        copies[-1].start()
    for copy in copies:
        copy.wait()


def arrange(packing_list, masked, pieces):
    groups = len(pieces)
    return pl.pallas_call(
        functools.partial(arrange_kernel, groups),
        out_shape=jax.ShapeDtypeStruct(masked.shape, jnp.bfloat16),
        in_specs=vmem(groups + 2),
        out_specs=anywhere(1)[0],
        scratch_shapes=[
            pltpu.VMEM(masked.shape, jnp.bfloat16),
            pltpu.SemaphoreType.DMA((groups,)),
        ],
        compiler_params=params(),
        cost_estimate=cost(0.5),
        name="arrange",
    )(packing_list.reshape(1, groups), masked, *pieces)


def hold_kernel(*refs):
    pass


def hold(members, *behind, us=0.1):
    count = len(members)
    return tuple(
        pl.pallas_call(
            hold_kernel,
            out_shape=[jax.ShapeDtypeStruct(member.shape, member.dtype) for member in members],
            in_specs=anywhere(count + len(behind)),
            out_specs=anywhere(count),
            input_output_aliases={i: i for i in range(count)},
            compiler_params=params(),
            cost_estimate=cost(us),
            name="hold",
        )(*members, *behind)
    )


def exchange(pieces):
    groups = len(pieces)
    return [pieces[0]] + [
        lax.ppermute(pieces[r], "group", [(i, i ^ r) for i in range(groups)])
        for r in range(1, groups)
    ]


def on_device(
    series, recon_mask, mask_token, packing_list, doc_ids, norm_gain, w_query, w_key, w_value, w_out
):
    groups, shards = lax.axis_size("group"), lax.axis_size("ctx")
    rows, width = series.shape
    piece = rows // groups
    ring = list(range(0, shards, 2)) + list(range(shards - 1, 0, -2))
    onward = [(ring[i], ring[(i + 1) % shards]) for i in range(shards)]
    backward = [(there, here) for here, there in onward]

    half = rows // 2
    sent, masked = route(
        packing_list, series, recon_mask, mask_token, norm_gain, doc_ids, groups
    )
    w_query, w_key, w_value = stage((w_query, w_key, w_value), 2, sent[0], 0.01)
    pieces = exchange(sent)
    low = groups // 2
    spans = [(r, 0, piece) for r in range(low)]
    a = join(pieces[:low], spans + [(0, piece, 8)])
    b = join(pieces[low:], spans, (a, w_value))

    def onto(member):
        return lax.ppermute(member, "ctx", onward)

    def back(member):
        return lax.ppermute(member, "ctx", backward)

    own_layout = ([(0, 0, half), (1, 0, half)], (0, half))
    pair_layout = (own_layout, ([(2, 0, half), (3, 0, half)], (2, half)))
    far_layout = (own_layout,)
    queries, state = own_call((a, b), own_layout, w_query, w_key, w_value, piece, rows)
    a_before, a_after, b_before, b_after = a, a, b, b
    for step in range(1, shards // 2):
        a_before, a_after = hold((onto(a_before), back(a_after)), state, us=AH)
        b_before, b_after = hold((onto(b_before), back(b_after)), us=BH)
        received = (a_before, b_before, a_after, b_after)
        state = chunk_call(queries, w_key, w_value, state, received, pair_layout, piece)
    far = (onto(a_before), back(b_after))
    done = last_call(queries, w_key, w_value, state, w_out, far, far_layout, groups, piece)
    return arrange(packing_list, masked, exchange(done))


def solution(mesh):
    in_specs = (
        P(("group", "ctx"), None),
        P(("group", "ctx")),
        P(),
        P(("group", "ctx")),
        P("group", "ctx"),
        P(),
        P(),
        P(),
        P(),
        P(),
    )
    out_specs = P(("group", "ctx"), None)
    return jax.shard_map(
        on_device, mesh=mesh, in_specs=in_specs, out_specs=out_specs, check_vma=False
    )
```

```python
import functools
import math

import jax
import jax.numpy as jnp
from jax import lax
from jax.experimental import pallas as pl
from jax.experimental.pallas import tpu as pltpu
from jax.sharding import PartitionSpec as P

HEADS = 12
AH = 0.1
BH = 0.1
HD = 64
STEP_HEADS = 4
STEP_COLS = STEP_HEADS * HD
STATE_ROWS = HD + 16
BIG = 3.3895313892515355e38
LARGEST = 1e30
LOG2E = 1.4426950408889634
COST = 0.05 * 1.1e9
LARGE = 56 * 1024 * 1024
VMEM_LIMIT = 32 * 1024 * 1024


def vmem(count):
    return [pl.BlockSpec(memory_space=pltpu.VMEM)] * count


def hbm(count):
    return [pl.BlockSpec(memory_space=pltpu.HBM)] * count


def anywhere(count):
    return [pl.BlockSpec(memory_space=pl.ANY)] * count


def smem():
    return pl.BlockSpec(memory_space=pltpu.SMEM)


def params(limit=VMEM_LIMIT):
    return pltpu.CompilerParams(vmem_limit_bytes=limit)


def cost(us):
    return pl.CostEstimate(flops=int(us * COST), bytes_accessed=0, transcendentals=0)


def piece_of(listing_ref, group, groups):
    place = jnp.int32(0)
    for k in range(groups):
        place = place + jnp.where(listing_ref[k] == group, jnp.int32(k), jnp.int32(0))
    return place


def fill_masked(mask_ref, token_ref, series_ref, masked_ref):
    width = series_ref.shape[1]
    token = token_ref[...].reshape(1, width)
    for part in range(mask_ref.shape[0]):
        line = mask_ref[part : part + 1, :].astype(jnp.float32)
        hidden = jnp.broadcast_to(line, (128, 128)).T > 0.5
        here = slice(part * 128, (part + 1) * 128)
        for lane in range(0, width, 128):
            masked_ref[here, lane : lane + 128] = jnp.where(
                hidden,
                token[:, lane : lane + 128].astype(jnp.float32),
                series_ref[here, lane : lane + 128].astype(jnp.float32),
            ).astype(jnp.bfloat16)


def masked_kernel(mask_ref, token_ref, series_ref, behind_ref, masked_ref):
    fill_masked(mask_ref, token_ref, series_ref, masked_ref)


def masked_rows(series, recon_mask, mask_token, behind):
    rows = series.shape[0]
    return pl.pallas_call(
        masked_kernel,
        out_shape=jax.ShapeDtypeStruct(series.shape, jnp.bfloat16),
        in_specs=vmem(3) + anywhere(1),
        out_specs=vmem(1)[0],
        compiler_params=params(),
        cost_estimate=cost(0.1),
        name="masked_rows",
    )(recon_mask.reshape(rows // 128, 128), mask_token, series, behind)


def route_kernel(
    groups, from_ref, series_ref, mask_ref, token_ref, gain_ref, docs_ref, *rest
):
    out_refs = rest[:groups]
    listing_ref, held_ref, lines_ref, word_ref, scale_ref, numbers_ref, masked_ref, sems = rest[
        groups:
    ]
    rows, width = series_ref.shape
    piece = rows // groups
    own = lax.axis_index("group")
    copies = [
        pltpu.make_async_copy(from_ref, listing_ref, sems.at[0]),
        pltpu.make_async_copy(mask_ref, lines_ref, sems.at[1]),
        pltpu.make_async_copy(token_ref, word_ref, sems.at[2]),
        pltpu.make_async_copy(series_ref, held_ref, sems.at[3]),
        pltpu.make_async_copy(gain_ref, scale_ref, sems.at[4]),
        pltpu.make_async_copy(docs_ref, numbers_ref, sems.at[5]),
    ]
    for copy in copies:
        copy.start()
    for copy in copies:
        copy.wait()
    fill_masked(lines_ref, word_ref, held_ref, masked_ref)
    gain = scale_ref[...].astype(jnp.float32).reshape(1, width)
    for r in range(groups):
        place = piece_of(listing_ref, lax.bitwise_xor(own, jnp.int32(r)), groups)
        widened = masked_ref[pl.ds(pl.multiple_of(place * piece, piece), piece), :].astype(jnp.float32)
        factor = lax.rsqrt(jnp.mean(widened * widened, axis=-1, keepdims=True) + 1e-06)
        out_refs[r][:piece, :] = (widened * factor * gain).astype(jnp.bfloat16)
    row = lax.broadcasted_iota(jnp.int32, (8, width), 0)
    lines = jnp.zeros((8, width), jnp.float32)
    for d in (1, 2, 3):
        below = jnp.sum(jnp.where(numbers_ref[...] < d, 1.0, 0.0), axis=-1, keepdims=True)
        lines = jnp.where(row == d, below, lines)
    out_refs[0][piece:, :] = lines.astype(jnp.bfloat16)


def route(packing_list, series, recon_mask, mask_token, norm_gain, doc_ids, groups):
    rows, width = series.shape
    piece = rows // groups
    return pl.pallas_call(
        functools.partial(route_kernel, groups),
        out_shape=[
            jax.ShapeDtypeStruct((piece + 8 if r == 0 else piece, width), jnp.bfloat16)
            for r in range(groups)
        ],
        in_specs=anywhere(6),
        out_specs=vmem(groups),
        scratch_shapes=[
            pltpu.SMEM((groups,), jnp.int32),
            pltpu.VMEM((rows, width), jnp.bfloat16),
            pltpu.VMEM((rows // 128, 128), jnp.int32),
            pltpu.VMEM((width,), jnp.bfloat16),
            pltpu.VMEM((width,), jnp.bfloat16),
            pltpu.VMEM(doc_ids.shape, jnp.int32),
            pltpu.VMEM((rows, width), jnp.bfloat16),
            pltpu.SemaphoreType.DMA((6,)),
        ],
        compiler_params=params(LARGE),
        cost_estimate=cost(100.0),
        name="route",
    )(
        packing_list,
        series,
        recon_mask.reshape(rows // 128, 128),
        mask_token,
        norm_gain,
        doc_ids,
    )


def stage_kernel(count, turned, *refs):
    from_refs, to_refs = refs[:count], refs[count + 1 : 2 * count + 1]
    scratch, sems = refs[2 * count + 1 : -1], refs[-1]
    copies = []
    for i in range(count):
        target = scratch[0] if i == turned else to_refs[i]
        copies.append(pltpu.make_async_copy(from_refs[i], target, sems.at[i]))
    for copy in copies:
        copy.start()
    for copy in copies:
        copy.wait()
    if turned is not None:
        width = to_refs[turned].shape[0]
        for lane in range(0, width, 256):
            to_refs[turned][lane : lane + 256, :] = (
                scratch[0][:, lane : lane + 256].astype(jnp.float32).T.astype(jnp.bfloat16)
            )


def stage(weights, turned, behind, us):
    count = len(weights)
    scratch = [pltpu.VMEM(weights[turned].shape, jnp.bfloat16)] if turned is not None else []
    return pl.pallas_call(
        functools.partial(stage_kernel, count, turned),
        out_shape=[jax.ShapeDtypeStruct(member.shape, member.dtype) for member in weights],
        in_specs=hbm(count) + anywhere(1),
        out_specs=vmem(count),
        scratch_shapes=scratch + [pltpu.SemaphoreType.DMA((count,))],
        compiler_params=params(),
        cost_estimate=cost(us),
        name="stage",
    )(*weights, behind)


def join_kernel(spans, *refs):
    out_ref, at = refs[-1], 0
    for i, first, count in spans:
        out_ref[at : at + count, :] = refs[i][first : first + count, :]
        at += count


def join(members, spans, behind=()):
    rows, width = sum(count for _, _, count in spans), members[0].shape[1]
    return pl.pallas_call(
        functools.partial(join_kernel, spans),
        out_shape=jax.ShapeDtypeStruct((rows, width), jnp.bfloat16),
        in_specs=vmem(len(members)) + anywhere(len(behind)),
        out_specs=vmem(1)[0],
        compiler_params=params(),
        cost_estimate=cost(0.2),
        name="join",
    )(*members, *behind)


def borders_of(ref, first):
    return ref[first : first + 8, :].astype(jnp.float32)


def places_of(count, piece, shape, axis):
    own = lax.axis_index("group")
    held = lax.broadcasted_iota(jnp.int32, shape, axis)
    return lax.bitwise_xor(held, own * piece).astype(jnp.float32)


def doc_numbers(borders, place):
    docs = jnp.zeros(place.shape, jnp.float32)
    for d in (1, 2, 3):
        docs = docs + jnp.where(place >= borders[d : d + 1, : place.shape[1]], 1.0, 0.0)
    return docs


def key_extras(borders, rows, piece):
    docs = doc_numbers(borders, places_of(rows, piece, (rows, 128), 0))
    column = lax.bitwise_and(lax.broadcasted_iota(jnp.int32, (rows, 128), 1), HD - 1)
    named = jnp.where(docs == column.astype(jnp.float32), 1.0, 0.0)
    flags = jnp.where(column < 7, 1.0, 0.0)
    return jnp.where(column < 4, named, flags).astype(jnp.bfloat16)


def load_rows(parts):
    return jnp.concatenate([ref[first : first + count, :] for ref, first, count in parts], axis=0)


def scores_of(keys, extras, queries):
    low = lax.broadcasted_iota(jnp.int32, extras.shape, 1) < HD
    scores = []
    for h in range(STEP_HEADS):
        pair = keys[:, h // 2 * 128 : h // 2 * 128 + 128]
        mixed = jnp.where(low, pair, extras) if h % 2 == 0 else jnp.where(low, extras, pair)
        scores.append(jnp.dot(mixed, queries[h], preferred_element_type=jnp.float32))
    return scores


def with_ones(values, h):
    ones = jnp.ones((16, values.shape[1]), jnp.bfloat16)
    return jnp.concatenate([values[h * HD : (h + 1) * HD], ones], axis=0)


def project(x, weight_ref, j):
    columns = weight_ref[:, j * STEP_COLS : (j + 1) * STEP_COLS]
    return jnp.dot(x, columns, preferred_element_type=jnp.float32)


def project_turned(x, weight_ref, j):
    return lax.dot_general(
        weight_ref[j * STEP_COLS : (j + 1) * STEP_COLS, :],
        x,
        (((1,), (1,)), ((), ())),
        preferred_element_type=jnp.float32,
    ).astype(jnp.bfloat16)


def own_kernel(piece, parts, borders_at, *refs):
    row_refs, (wq_ref, wk_ref, wv_ref, queries_ref, state_ref) = refs[:-5], refs[-5:]
    x = load_rows([(row_refs[i], first, count) for i, first, count in parts])
    rows = x.shape[0]
    borders = borders_of(row_refs[borders_at[0]], borders_at[1])
    docs = doc_numbers(borders, places_of(rows, piece, (8, rows), 1))
    row = lax.broadcasted_iota(jnp.int32, (HD, rows), 0)
    differs = jnp.where(docs[0:1, :] == row.astype(jnp.float32), 0.0, -BIG)
    mask_rows = jnp.where(row < 4, differs, 0.0)
    extras = key_extras(borders, rows, piece)
    for j in range(HEADS // STEP_HEADS):
        queries = project(x, wq_ref, j).astype(jnp.bfloat16).astype(jnp.float32)
        queries = (queries * (1.0 / math.sqrt(HD))).T.astype(jnp.bfloat16)
        keys = project(x, wk_ref, j).astype(jnp.bfloat16)
        values = project_turned(x, wv_ref, j)

        def stacked(h, rest):
            own = queries[h * HD : (h + 1) * HD]
            return jnp.concatenate([own, rest] if h % 2 == 0 else [rest, own], axis=0)

        plain = mask_rows.astype(jnp.bfloat16)
        scores = scores_of(keys, extras, [stacked(h, plain) for h in range(STEP_HEADS)])
        tops = [jnp.max(member, axis=0, keepdims=True) for member in scores]
        weights = [
            jnp.exp2((member - top) * LOG2E).astype(jnp.bfloat16)
            for member, top in zip(scores, tops)
        ]
        sums = [
            jnp.dot(with_ones(values, h), weights[h], preferred_element_type=jnp.float32)
            for h in range(STEP_HEADS)
        ]
        for h in range(STEP_HEADS):
            upper = tops[h].astype(jnp.bfloat16).astype(jnp.float32)
            middle = (tops[h] - upper).astype(jnp.bfloat16).astype(jnp.float32)
            lower = tops[h] - upper - middle
            rest = jnp.where(row == 4, -upper, mask_rows)
            rest = jnp.where(row == 5, -middle, rest)
            rest = jnp.where(row == 6, -lower, rest)
            queries_ref[j * STEP_HEADS + h] = stacked(h, rest.astype(jnp.bfloat16))
            state_ref[j * STEP_HEADS + h, : HD + 8, :] = sums[h][: HD + 8]
            state_ref[j * STEP_HEADS + h, HD + 8 :, :] = jnp.zeros((8, rows), jnp.float32)


def fold(piece, sources, queries_ref, wk_ref, wv_ref, state_ref, finish):
    x = jnp.concatenate([load_rows(parts) for parts, _, _ in sources], axis=0)
    extras = jnp.concatenate(
        [
            key_extras(borders_of(ref, first), sum(count for _, _, count in parts), piece)
            for parts, ref, first in sources
        ],
        axis=0,
    )
    largest, excess = [], []
    for j in range(HEADS // STEP_HEADS):
        heads = [j * STEP_HEADS + h for h in range(STEP_HEADS)]
        keys = project(x, wk_ref, j).astype(jnp.bfloat16)
        values = project_turned(x, wv_ref, j)
        scores = scores_of(keys, extras, [queries_ref[head] for head in heads])
        weights = [jnp.exp2(member * LOG2E).astype(jnp.bfloat16) for member in scores]
        sums = [
            state_ref[head, : HD + 8, :]
            + jnp.dot(with_ones(values, h), weights[h], preferred_element_type=jnp.float32)[: HD + 8]
            for h, head in enumerate(heads)
        ]
        for h, head in enumerate(heads):
            finish(head, sums[h], None)
            largest.append(sums[h][HD : HD + 8])
            excess.append(state_ref[head, HD + 8 :, :])
    largest = functools.reduce(jnp.maximum, largest)
    excess = functools.reduce(jnp.maximum, excess)
    usual = jnp.logical_and(largest < LARGEST, excess <= 0.0)

    @pl.when(jnp.min(jnp.where(usual, 1.0, 0.0)) < 0.5)
    def again():
        for j in range(HEADS // STEP_HEADS):
            heads = [j * STEP_HEADS + h for h in range(STEP_HEADS)]
            keys = project(x, wk_ref, j).astype(jnp.bfloat16)
            values = project_turned(x, wv_ref, j)
            scores = scores_of(keys, extras, [queries_ref[head] for head in heads])
            for h, head in enumerate(heads):
                before = state_ref[head, HD + 8 : HD + 9, :]
                top = jnp.maximum(before, jnp.max(scores[h], axis=0, keepdims=True))
                weights = jnp.exp2((scores[h] - top) * LOG2E).astype(jnp.bfloat16)
                added = jnp.dot(with_ones(values, h), weights, preferred_element_type=jnp.float32)
                factor = jnp.exp2((before - top) * LOG2E)
                finish(
                    head,
                    state_ref[head, : HD + 8, :] * factor + added[: HD + 8],
                    jnp.broadcast_to(top, (8, top.shape[1])),
                )


def named_sources(row_refs, layout):
    return [
        ([(row_refs[i], first, count) for i, first, count in parts], row_refs[at], first_border)
        for parts, (at, first_border) in layout
    ]


def chunk_kernel(piece, layout, queries_ref, wk_ref, wv_ref, old_ref, *rest):
    row_refs, state_ref = rest[:-1], rest[-1]

    def finish(head, sums, top):
        state_ref[head, : HD + 8, :] = sums
        state_ref[head, HD + 8 :, :] = jnp.zeros((8, sums.shape[1]), jnp.float32) if top is None else top

    fold(piece, named_sources(row_refs, layout), queries_ref, wk_ref, wv_ref, old_ref, finish)


def last_kernel(groups, piece, layout, queries_ref, wk_ref, wv_ref, old_ref, wo_ref, *rest):
    row_refs, out_refs = rest[: -groups - 1], rest[-groups - 1 : -1]
    attended_ref = rest[-1]

    def finish(head, sums, top):
        attended_ref[head * HD : (head + 1) * HD, :] = sums[:HD] / sums[HD : HD + 1]

    fold(piece, named_sources(row_refs, layout), queries_ref, wk_ref, wv_ref, old_ref, finish)
    attended = attended_ref[...].T.astype(jnp.bfloat16)
    mixed = jnp.dot(attended, wo_ref[...], preferred_element_type=jnp.float32)
    for r in range(groups):
        out_refs[r][...] = mixed[r * piece : (r + 1) * piece].astype(jnp.bfloat16)


def own_call(members, layout, w_query, w_key, w_value, piece, rows):
    parts, borders_at = layout
    return pl.pallas_call(
        functools.partial(own_kernel, piece, parts, borders_at),
        out_shape=[
            jax.ShapeDtypeStruct((HEADS, 2 * HD, rows), jnp.bfloat16),
            jax.ShapeDtypeStruct((HEADS, STATE_ROWS, rows), jnp.float32),
        ],
        in_specs=vmem(len(members) + 3),
        out_specs=vmem(2),
        compiler_params=params(),
        cost_estimate=cost(3.0),
        name="own_rows",
    )(*members, w_query, w_key, w_value)


def chunk_call(queries, w_key, w_value, state, members, layout, piece):
    return pl.pallas_call(
        functools.partial(chunk_kernel, piece, layout),
        out_shape=jax.ShapeDtypeStruct(state.shape, jnp.float32),
        in_specs=vmem(4 + len(members)),
        out_specs=vmem(1)[0],
        compiler_params=params(),
        cost_estimate=cost(3.5),
        name="received_rows",
    )(queries, w_key, w_value, state, *members)


def last_call(queries, w_key, w_value, state, w_out, members, layout, groups, piece):
    width = w_key.shape[0]
    rows = queries.shape[2]
    return pl.pallas_call(
        functools.partial(last_kernel, groups, piece, layout),
        out_shape=[jax.ShapeDtypeStruct((piece, width), jnp.bfloat16)] * groups,
        in_specs=vmem(5 + len(members)),
        out_specs=vmem(groups),
        scratch_shapes=[pltpu.VMEM((HEADS * HD, rows), jnp.float32)],
        compiler_params=params(),
        cost_estimate=cost(3.0),
        name="last_rows",
    )(queries, w_key, w_value, state, w_out, *members)


def arrange_kernel(groups, listing_ref, masked_ref, *refs):
    piece_refs, out_ref, sums_ref, sems = refs[:groups], refs[-3], refs[-2], refs[-1]
    piece = piece_refs[0].shape[0]
    own = lax.axis_index("group")
    copies = []
    for k in range(groups):
        group = listing_ref[0:1, k : k + 1]
        here = slice(k * piece, (k + 1) * piece)
        back = piece_refs[0][...].astype(jnp.float32)
        for r in range(1, groups):
            mine = group == lax.bitwise_xor(own, jnp.int32(r))
            back = jnp.where(mine, piece_refs[r][...].astype(jnp.float32), back)
        sums_ref[here, :] = (masked_ref[here, :].astype(jnp.float32) + back).astype(jnp.bfloat16)
        copies.append(pltpu.make_async_copy(sums_ref.at[here, :], out_ref.at[here, :], sems.at[k]))
        copies[-1].start()
    for copy in copies:
        copy.wait()


def arrange(packing_list, masked, pieces):
    groups = len(pieces)
    return pl.pallas_call(
        functools.partial(arrange_kernel, groups),
        out_shape=jax.ShapeDtypeStruct(masked.shape, jnp.bfloat16),
        in_specs=vmem(groups + 2),
        out_specs=anywhere(1)[0],
        scratch_shapes=[
            pltpu.VMEM(masked.shape, jnp.bfloat16),
            pltpu.SemaphoreType.DMA((groups,)),
        ],
        compiler_params=params(),
        cost_estimate=cost(0.5),
        name="arrange",
    )(packing_list.reshape(1, groups), masked, *pieces)


def hold_kernel(*refs):
    pass


def hold(members, *behind, us=0.1):
    count = len(members)
    return tuple(
        pl.pallas_call(
            hold_kernel,
            out_shape=[jax.ShapeDtypeStruct(member.shape, member.dtype) for member in members],
            in_specs=anywhere(count + len(behind)),
            out_specs=anywhere(count),
            input_output_aliases={i: i for i in range(count)},
            compiler_params=params(),
            cost_estimate=cost(us),
            name="hold",
        )(*members, *behind)
    )


def exchange(pieces):
    groups = len(pieces)
    return [pieces[0]] + [
        lax.ppermute(pieces[r], "group", [(i, i ^ r) for i in range(groups)])
        for r in range(1, groups)
    ]


def on_device(
    series, recon_mask, mask_token, packing_list, doc_ids, norm_gain, w_query, w_key, w_value, w_out
):
    groups, shards = lax.axis_size("group"), lax.axis_size("ctx")
    rows, width = series.shape
    piece = rows // groups
    ring = list(range(0, shards, 2)) + list(range(shards - 1, 0, -2))
    onward = [(ring[i], ring[(i + 1) % shards]) for i in range(shards)]
    backward = [(there, here) for here, there in onward]

    half = rows // 2
    sent = route(
        packing_list, series, recon_mask, mask_token, norm_gain, doc_ids, groups
    )
    w_query, w_key, w_value = stage((w_query, w_key, w_value), 2, sent[0], 0.01)
    pieces = exchange(sent)
    low = groups // 2
    spans = [(r, 0, piece) for r in range(low)]
    a = join(pieces[:low], spans + [(0, piece, 8)])
    masked = masked_rows(series, recon_mask, mask_token, w_value)
    b = join(pieces[low:], spans, (a, w_value, masked))

    def onto(member):
        return lax.ppermute(member, "ctx", onward)

    def back(member):
        return lax.ppermute(member, "ctx", backward)

    own_layout = ([(0, 0, half), (1, 0, half)], (0, half))
    pair_layout = (own_layout, ([(2, 0, half), (3, 0, half)], (2, half)))
    far_layout = (own_layout,)
    queries, state = own_call((a, b), own_layout, w_query, w_key, w_value, piece, rows)
    a_before, a_after, b_before, b_after = a, a, b, b
    for step in range(1, shards // 2):
        a_before, a_after = hold((onto(a_before), back(a_after)), state, us=AH)
        b_before, b_after = hold((onto(b_before), back(b_after)), us=BH)
        received = (a_before, b_before, a_after, b_after)
        state = chunk_call(queries, w_key, w_value, state, received, pair_layout, piece)
    far = (onto(a_before), back(b_after))
    done = last_call(queries, w_key, w_value, state, w_out, far, far_layout, groups, piece)
    return arrange(packing_list, masked, exchange(done))


def solution(mesh):
    in_specs = (
        P(("group", "ctx"), None),
        P(("group", "ctx")),
        P(),
        P(("group", "ctx")),
        P("group", "ctx"),
        P(),
        P(),
        P(),
        P(),
        P(),
    )
    out_specs = P(("group", "ctx"), None)
    return jax.shard_map(
        on_device, mesh=mesh, in_specs=in_specs, out_specs=out_specs, check_vma=False
    )
```
